32 devices in a mesh: vocab: 4 (over y, x), docs: 8 (over z, core).
Axes of the slice: x: 2, y: 2, z: 4, core: 2. Of those that a mesh axis runs over, the one named last changes fastest.
Arguments:
- hidden: bfloat16 [24, 256, 2048], P('docs', 'vocab'), may hold values from -6 to 6
- w_vocab: bfloat16 [16384, 2048], P(('vocab', 'docs')), may hold values from -0.125 to 0.125
- lengths: int32 [24], P('docs'), may hold values from 1 to 256, as said below
- query_terms: bfloat16 [1024, 16384], P('docs', 'vocab'), may hold values from -0.09375 to 0.09375
- tile_routes: int32 [8, 128, 4], P('docs', 'vocab'), may hold values from 0 to 7, all different within a row; in each aligned block of 32 rows (0 to 31, 32 to 63, ..., all dimensions but the last counted through in order) at most 32 rows name the same one
Outputs:
- doc_terms: bfloat16 [24, 16384], P('docs', 'vocab')
- scores: float32 [1024, 24], P('docs', 'vocab')
The draws below stay inside these ranges and needn't reach their ends.
Inputs may be any that keep to these rules, and one draw needn't show every extreme that they name: `lengths`: the last passage has 256 tokens. `tile_routes`: each row names 4 different query tiles; among the 32 rows of one device no query tile is named more than 32 times.
All inputs are finite; a program needn't handle non-finite values.
Results may differ from the reference program's by a relative error of at most 0.009.
Values may be sent and summed in bfloat16 or wider, within the bound.
A program may use at most 384 MiB of HBM per device.

```python
import math
import jax
import jax.numpy as jnp
import numpy as np
from jax import lax

D = 2048
V = 16384
S = 256
TILE = 128
QT = 128
TOP = 4
P_DEV = 3
PASSAGES = 24
NQ = 1024
TT = 128
TT_DEV = 32
CAP = 32
N_DOCS = 8


def draw_hidden(key, part):
    key_common, key_noise = jax.random.split(jax.random.fold_in(key, 11), 2)
    common = jax.random.normal(key_common, (PASSAGES, 1, D), jnp.float32)
    noise = jax.random.normal(key_noise, (PASSAGES, S, D), jnp.float32)
    values = common + 0.7 * noise
    return jnp.clip(values, -6.0, 6.0).astype(jnp.bfloat16)


def draw_lengths(key, part):
    places = jnp.arange(PASSAGES, dtype=jnp.int32)
    lowest = max(S // 16, 1)
    upper_end = S // 4 + (S - S // 4) * places // max(PASSAGES - 1, 1)
    raw_bits = jax.random.randint(jax.random.fold_in(key, 23), (PASSAGES,), 0, 1 << 20, jnp.int32)
    drawn = lowest + raw_bits % (upper_end - lowest + 1)
    return jnp.where(places == PASSAGES - 1, S, drawn).astype(jnp.int32)


def block_scale(rng, shape, shards, smallest, high):
    factor_of = 1.0
    for axis_at, blocks in shards:
        steps = jax.random.uniform(jax.random.fold_in(jax.random.fold_in(rng, 6), axis_at), (blocks,), jnp.float32, smallest / len(shards), high / len(shards))
        factor_of = factor_of * jnp.repeat(jnp.exp(steps), shape[axis_at] // blocks).reshape((-1,) + (1,) * (len(shape) - 1 - axis_at))
    return factor_of


def assign_block(key, own, number, rows, amount, top, reach, lean):
    ranking = jax.random.permutation(key, amount)
    crowded, usual = shares(amount, rows * top, reach, lean, True), shares(amount, rows * top, reach, lean, False)
    places = jnp.arange(amount)

    def named(sizes, rotation):
        used = int((sizes > 0).sum())
        fixed = max(1, used // 4)
        moved = fixed + (places - fixed + rotation * (used - fixed)) % max(1, amount - fixed)
        return jnp.zeros((amount,), jnp.int32).at[ranking[jnp.where(places < fixed, places, moved)]].set(jnp.asarray(sizes, jnp.int32))

    sizes = jnp.where(number % 4 == 0, named(crowded, number // 4), named(usual, number - number // 4 - 1))
    mixed = jax.random.permutation(jax.random.fold_in(own, 3), amount)
    giver, taker = mixed[0:amount // 2 * 2:2], mixed[1:amount // 2 * 2:2]
    room = jnp.minimum(sizes[giver] - 1, reach - sizes[taker]) // 2
    room = jnp.where((giver == ranking[0]) | (taker == ranking[0]) | (sizes[taker] == 0), 0, jnp.maximum(room, 0))
    moved = jax.random.randint(jax.random.fold_in(own, 4), (amount // 2,), 0, 1 << 20) % (room + 1)
    sizes = sizes.at[giver].add(-moved).at[taker].add(moved)
    members = jnp.searchsorted(jnp.cumsum(sizes), jnp.arange(rows * top), side="right").astype(jnp.int32)
    listing = members.reshape(top, rows).T
    listing = listing[jax.random.permutation(jax.random.fold_in(own, 1), rows)]
    rotation = jax.random.randint(jax.random.fold_in(own, 2), (rows, 1), 0, top)
    return jnp.take_along_axis(listing, (jnp.arange(top)[None, :] + rotation) % top, axis=1)


def shares(number_of, total, limit, slope, full):
    weights = [(1 << 20) // math.isqrt(grade ** slope) + 1 for grade in range(1, number_of + 1)]
    largest = limit if full else min(limit, max(-(-total // number_of), total * weights[0] // sum(weights)))
    least = 1 if total - largest >= number_of - 1 else 0
    holding, rest = [largest] + [least] * (number_of - 1), total - largest - least * (number_of - 1)
    while rest > 0:
        candidates = [i for i in range(1, number_of) if holding[i] < largest] or [i for i in range(1, number_of) if holding[i] < limit]
        whole, budget = sum([weights[i] for i in candidates]), rest
        for i in candidates:
            extra = min(limit - holding[i], max(1, budget * weights[i] // whole), rest)
            holding[i] = holding[i] + extra
            rest = rest - extra
    return np.array(holding)


def centred(own_key, extent, spread, most, pieces=(), held_as=jnp.bfloat16):
    values = spread * jax.random.normal(own_key, extent, jnp.float32)
    if pieces:
        values = values * block_scale(own_key, extent, pieces, -0.22, 0.18)
    return jnp.clip(values, -most, most).astype(held_as)


def setup_inputs(seed: int = 0) -> dict:
    key_list = jax.random.split(jax.random.key(seed), 6)
    hidden = draw_hidden(jax.random.fold_in(key_list[5], 71), 0)
    w_vocab = centred(key_list[1], (V, D), D ** -0.5, 0.125, ((0, 32),))
    lengths = draw_lengths(jax.random.fold_in(key_list[5], 71), 0)
    query_terms = centred(key_list[3], (NQ, V), (0.6 * (TT * TOP * TILE // N_DOCS) ** -0.5), 0.09375, ((0, 8), (1, 4)))
    tile_routes_keys = jax.random.split(jax.random.fold_in(key_list[4], 1), N_DOCS * TT // TT_DEV)
    tile_routes_turns = jax.random.permutation(jax.random.fold_in(key_list[4], 3), N_DOCS * TT // TT_DEV)
    tile_routes = jax.vmap(lambda own, number: assign_block(jax.random.fold_in(key_list[4], 2), own, number, TT_DEV, N_DOCS, TOP, CAP, 2))(tile_routes_keys, tile_routes_turns).reshape((N_DOCS, TT, TOP))
    return {"hidden": hidden, "w_vocab": w_vocab, "lengths": lengths, "query_terms": query_terms, "tile_routes": tile_routes}


saturate = 1.2
length_slope = 0.75


def reference(hidden, w_vocab, lengths, query_terms, tile_routes):
    lens_f = lengths.astype(jnp.float32)
    average = jnp.sum(lens_f) / PASSAGES

    def pool_one(inputs_pair):
        passage_rows, length_one = inputs_pair
        logits = jnp.dot(passage_rows, w_vocab.T, preferred_element_type=jnp.float32)
        valid_pos = jnp.arange(S, dtype=jnp.int32) < length_one
        activity = jnp.where(valid_pos[:, None], jnp.log1p(jnp.maximum(logits, 0.0)), 0.0)
        return jnp.sum(activity, axis=0) / length_one.astype(jnp.float32)

    pooled = lax.map(pool_one, (hidden, lengths))
    doc_terms = pooled.astype(jnp.bfloat16)
    weight = doc_terms.astype(jnp.float32)
    denominator = saturate * (1.0 - length_slope + length_slope * lens_f / average)
    scaled = (weight * (saturate + 1.0) / (weight + denominator[:, None])).astype(jnp.bfloat16)
    blocks = scaled.reshape(N_DOCS, P_DEV, TT, TILE)

    def score_tile(tile_index):
        listed = jnp.any(tile_routes == tile_index, axis=2)
        masked = (blocks * listed[:, None, :, None].astype(jnp.bfloat16)).reshape(PASSAGES, V)
        query_rows = lax.dynamic_slice_in_dim(query_terms, tile_index * QT, QT, 0)
        return lax.dot_general(query_rows, masked, (((1,), (1,)), ((), ())), preferred_element_type=jnp.float32)

    scores = lax.map(score_tile, jnp.arange(N_DOCS, dtype=jnp.int32)).reshape(NQ, PASSAGES)
    return doc_terms, scores
```

```python
import jax
import jax.numpy as jnp
from jax import lax
from jax.experimental import pallas as pl
from jax.experimental.pallas import tpu as pltpu
from jax.sharding import PartitionSpec as P

saturate = 1.2
length_slope = 0.75


def pooled_rows(passage_rows, weights, lens_here):
    logits = lax.dot_general(
        passage_rows, weights, (((2,), (1,)), ((), ())), preferred_element_type=jnp.float32
    )
    places = lax.broadcasted_iota(jnp.int32, logits.shape, 1)
    activity = jnp.where(
        places < lens_here[:, None, None], jnp.log1p(jnp.maximum(logits, 0.0)), 0.0
    )
    return jnp.sum(activity, axis=1) / lens_here.astype(jnp.float32)[:, None]


def local(hidden, w_vocab, lengths, query_terms, tile_routes):
    members = lax.axis_size("docs")
    local_count = hidden.shape[0]
    lens_all = lax.all_gather(lengths, "docs", axis=0, tiled=True)
    passage_total = lens_all.shape[0]
    average = jnp.sum(lens_all.astype(jnp.float32)) / passage_total
    full_rows = lax.all_gather(hidden, "vocab", axis=1, tiled=True)
    doc_terms = pooled_rows(
        full_rows, lax.all_gather(w_vocab, "docs", axis=0, tiled=True), lengths
    ).astype(jnp.bfloat16)
    weight = doc_terms.astype(jnp.float32)
    denominator = saturate * (
        1.0 - length_slope + length_slope * lengths.astype(jnp.float32) / average
    )
    scaled = (weight * (saturate + 1.0) / (weight + denominator[:, None])).astype(jnp.bfloat16)
    term_count = scaled.shape[1]
    tile_count = term_count // 128
    my_routes = tile_routes[0]
    fanout = my_routes.shape[1]
    capacity = min(tile_count, max(4, 2 * tile_count * fanout // members))
    owners = lax.broadcasted_iota(jnp.int32, (1, 1, members), 2)
    is_listed = jnp.any(my_routes[:, :, None] == owners, axis=1)
    slot_index = jnp.cumsum(is_listed.astype(jnp.int32), axis=0) - 1
    slot_ids = lax.broadcasted_iota(jnp.int32, (1, capacity, 1), 1)
    selector = (is_listed.T[:, None, :] & (slot_index.T[:, None, :] == slot_ids)).astype(
        jnp.bfloat16
    )
    blocks = scaled.reshape(local_count, tile_count, 128)
    outgoing = jnp.einsum(
        "oct,ptk->ocpk", selector, blocks, preferred_element_type=jnp.float32
    ).astype(jnp.bfloat16)
    tile_ids = lax.broadcasted_iota(jnp.float32, (1, 1, tile_count), 2)
    labels = jnp.sum(selector.astype(jnp.float32) * tile_ids, axis=2).astype(jnp.bfloat16)
    arrived, labels_in = (
        lax.all_to_all(outgoing, "docs", split_axis=0, concat_axis=0, tiled=True),
        lax.all_to_all(labels, "docs", split_axis=0, concat_axis=0, tiled=True),
    )
    placing = (labels_in.astype(jnp.float32)[:, :, None] == tile_ids).astype(jnp.bfloat16)
    masked = jnp.einsum(
        "bct,bcpk->bptk", placing, arrived, preferred_element_type=jnp.float32
    ).astype(jnp.bfloat16)
    masked = masked.reshape(passage_total, term_count)
    partial_value = lax.dot_general(
        query_terms, masked, (((1,), (1,)), ((), ())), preferred_element_type=jnp.float32
    )
    scores = lax.psum_scatter(partial_value, "vocab", scatter_dimension=1, tiled=True)
    return (doc_terms, scores)


CHUNK = 256
MESH = pl.DeviceIdType.MESH


def head_kernel(
    hidden, weights, queries, meta, doc_out, score_out,
    rows, terms, query_rows, meta_all, keep, pooled, doc_send, doc_all, masked, part, part_send, part_all,
    local_sem, xh_s, xh_r, w_s, w_r, up_s, down_s, z_r, y_s, y_r, sib_s, sib_r,
    meta_s, meta_r, doc_s, doc_r, part_s, part_r,
):
    v, d = lax.axis_index("vocab"), lax.axis_index("docs")
    x, y, z, c = v % 2, v // 2, d // 2, d % 2
    x_side, y_side = (2 * y + 1 - x, d), (2 * (1 - y) + x, d)
    x_cross, sibling = (2 * y + 1 - x, 2 * z + 1 - c), (v, 2 * z + 1 - c)
    above, below = (v, d + 2), (v, d - 2)

    def send(src, dst, s_sem, r_sem, to):
        return pltpu.make_async_remote_copy(
            src_ref=src, dst_ref=dst, send_sem=s_sem, recv_sem=r_sem, device_id=to, device_id_type=MESH
        )

    barrier = pltpu.get_barrier_semaphore()

    @pl.loop(0, 16)
    def _(i):
        peer_v, peer_d = 2 * y + i // 8, i % 8

        @pl.when(jnp.logical_or(peer_v != v, peer_d != d))
        def _():
            pl.semaphore_signal(barrier, inc=1, device_id=(peer_v, peer_d), device_id_type=MESH)

    for i in range(2):
        pl.semaphore_signal(barrier, inc=1, device_id=(2 * (1 - y) + i, d), device_id_type=MESH)
    pl.semaphore_wait(barrier, 17)

    def slot(m, vp):
        return rows.at[m, pl.ds(pl.multiple_of(vp * 64, 64), 64), :]

    def from_x(j):
        block = slot(z * 3 + j, v)
        return send(hidden.at[j], block, xh_s.at[j], xh_r.at[j], x_cross)

    def own_rows(j):
        return pltpu.make_async_copy(hidden.at[j], slot(z * 3 + j, 2 * y + c), local_sem.at[j])

    def own_terms(h):
        return pltpu.make_async_copy(
            weights.at[pl.ds(h * CHUNK, CHUNK), :], terms.at[x * 2 + h], local_sem.at[3 + h]
        )

    own_queries = pltpu.make_async_copy(queries, query_rows, local_sem.at[5])

    def side_terms(h):
        return send(weights.at[pl.ds(h * CHUNK, CHUNK), :], terms.at[x * 2 + h], w_s.at[h], w_r.at[h], x_side)

    def side_terms_in(h):
        return send(weights.at[pl.ds(h * CHUNK, CHUNK), :], terms.at[(1 - x) * 2 + h], w_s.at[h], w_r.at[h], x_side)

    def go_up(m):
        return send(slot(m, 2 * y + c), slot(m, 2 * y + c), up_s.at[m], z_r.at[m], above)

    def go_down(m):
        return send(slot(m, 2 * y + c), slot(m, 2 * y + c), down_s.at[m], z_r.at[m], below)

    def go_y(m):
        return send(slot(m, 2 * y + c), slot(m, 2 * y + c), y_s.at[m], y_r.at[m], y_side)

    def come_y(m):
        block = slot(m, 2 * (1 - y) + c)
        return send(block, block, y_s.at[m], y_r.at[m], y_side)

    def go_sibling(m, side):
        block = slot(m, 2 * side + c)
        return send(block, block, sib_s.at[m * 2 + side], sib_r.at[m * 2 + side], sibling)

    def come_sibling(m, side):
        block = slot(m, 2 * side + 1 - c)
        return send(block, block, sib_s.at[m * 2 + side], sib_r.at[m * 2 + side], sibling)

    straight = c == x

    @pl.when(straight)
    def _():
        for j in range(3):
            own_rows(j).start()

    @pl.when(jnp.logical_not(straight))
    def _():
        for j in range(3):
            from_x(j).start()

    def meta_to(i):
        peer = (d + i) % 8
        return send(meta, meta_all.at[d], meta_s.at[i], meta_r.at[d], (v, peer))

    def meta_from(i):
        peer = (d + i) % 8
        return send(meta, meta_all.at[peer], meta_s.at[i], meta_r.at[peer], (v, peer))

    @pl.loop(1, 8)
    def _(i):
        meta_to(i).start()

    meta_all[d] = meta[...]
    for h in range(2):
        own_terms(h).start()
    own_queries.start()
    pooled[...] = jnp.zeros_like(pooled)

    for j in range(3):
        @pl.when(straight)
        def _():
            own_rows(j).wait()

        @pl.when(jnp.logical_not(straight))
        def _():
            slot_in = slot(z * 3 + j, 2 * y + c)
            send(hidden.at[j], slot_in, xh_s.at[j], xh_r.at[j], x_cross).wait_recv()

        m = z * 3 + j

        @pl.when(z < 3)
        def _():
            go_up(m).start()

        @pl.when(z > 0)
        def _():
            go_down(m).start()

        go_y(m).start()
        go_sibling(m, y).start()

    for h in range(2):
        own_terms(h).wait()

    @pl.loop(1, 8)
    def _(i):
        meta_from(i).wait_recv()

    row_id = lax.broadcasted_iota(jnp.int32, (16, 128), 0)
    mine = d.astype(jnp.float32)
    for side in range(2):
        listed = jnp.zeros((16, 128), jnp.float32)
        for zp in range(4):
            routes = meta_all[2 * zp + side][0:4, :]
            hit = jnp.max(jnp.where(routes == mine, 1.0, 0.0), axis=0, keepdims=True)
            listed = jnp.where(row_id // 4 == zp, hit, listed)
        for t in range(32):
            keep[side, :, t * 128:(t + 1) * 128] = jnp.broadcast_to(listed[:, t:t + 1], (16, 128))

    def order(n):
        end = jnp.logical_or(z == 0, z == 3)
        step = n - 3
        end_z = jnp.where(z == 0, z + step // 3 + 1, z - step // 3 - 1)
        near = jnp.where(step % 2 == 0, z - 1, z + 1)
        mid_z = jnp.where(n < 9, near, jnp.where(z == 1, 3, 0))
        mid_j = jnp.where(n < 9, step // 2, n - 9)
        zp = jnp.where(n < 3, z, jnp.where(end, end_z, mid_z))
        j = jnp.where(n < 3, n, jnp.where(end, step % 3, mid_j))
        return zp, j

    place = lax.broadcasted_iota(jnp.int32, (8, CHUNK), 0).astype(jnp.float32)

    def pool(n, q):
        zp, j = order(n)
        m = zp * 3 + j
        logits = lax.dot_general(
            rows[m], terms[q], (((1,), (1,)), ((), ())), preferred_element_type=jnp.float32
        )
        length = meta_all[2 * zp + x, pl.ds(4 + j, 1), :]
        length = jnp.concatenate([length] * (CHUNK // 128), axis=1)
        room = length - place
        total = jnp.zeros((8, CHUNK), jnp.float32)
        for g in range(0, 32, 8):
            parts = [
                jnp.where(room > float(8 * i), jnp.maximum(logits[8 * i:8 * i + 8, :], 0.0), 0.0)
                for i in range(g, g + 8)
            ]
            while len(parts) > 1:
                parts = [a + b + a * b for a, b in zip(parts[0::2], parts[1::2])]
            total = total + jnp.log1p(parts[0])
        pooled[q, pl.ds(zp * 4 + j, 1), :] = jnp.sum(total, axis=0, keepdims=True) / length

    @pl.loop(0, 12)
    def _(n):
        k, j = n // 3 + 1, n % 3

        @pl.when(jnp.logical_and(n < 9, z - k >= 0))
        def _():
            m = (z - k) * 3 + j
            go_up(m).wait_recv()

            @pl.when(z < 3)
            def _():
                go_up(m).start()

            go_y(m).start()
            go_sibling(m, y).start()

        @pl.when(jnp.logical_and(n < 9, z + k <= 3))
        def _():
            m = (z + k) * 3 + j
            go_down(m).wait_recv()

            @pl.when(z > 0)
            def _():
                go_down(m).start()

            go_y(m).start()
            go_sibling(m, y).start()

        zp, jj = order(n)
        m = zp * 3 + jj
        come_y(m).wait_recv()
        go_sibling(m, 1 - y).start()

        @pl.when(n == 0)
        def _():
            for h in range(2):
                side_terms(h).start()

        come_sibling(m, 0).wait_recv()
        come_sibling(m, 1).wait_recv()

        for h, first in ((0, 6), (1, 10)):
            @pl.when(n == first)
            def _():
                side_terms_in(h).wait_recv()

        @pl.loop(0, 4)
        def _(i):
            first = jnp.where(i == 2, 6, jnp.where(i == 3, 10, 0))
            start = jnp.where(n == first, 0, n)
            stop = jnp.where(n >= first, n + 1, start)
            q = jnp.where(i < 2, x * 2 + i, (1 - x) * 2 + i - 2)

            def step(at, carry):
                pool(at, q)
                return carry

            lax.fori_loop(start, stop, step, 0)

    for side in range(2):
        for h in range(2):
            doc_send[side, :, h * CHUNK:(h + 1) * CHUNK] = pooled[side * 2 + h].astype(jnp.bfloat16)

    def doc_to(i):
        side, peer = i // 8, i % 8
        return send(doc_send.at[side], doc_all.at[x, d], doc_s.at[i], doc_r.at[x * 8 + d], (2 * y + side, peer))

    def doc_from(i):
        side, peer = i // 8, i % 8
        return send(doc_send.at[side], doc_all.at[side, peer], doc_s.at[i], doc_r.at[i], (2 * y + side, peer))

    def not_me(i):
        return i != x * 8 + d

    @pl.loop(0, 16)
    def _(i):
        @pl.when(not_me(i))
        def _():
            doc_to(i).start()

    doc_all[x, d] = doc_send[x]

    length_sum = jnp.zeros((1, 128), jnp.float32)
    for b in range(8):
        for j in range(3):
            length_sum = length_sum + meta_all[b, 4 + j:5 + j, :]
    average = length_sum / 24.0
    dens = []
    for side in range(2):
        length_of = jnp.zeros((16, 128), jnp.float32)
        for zp in range(4):
            for j in range(3):
                length_of = jnp.where(row_id == zp * 4 + j, meta_all[2 * zp + side, 4 + j:5 + j, :], length_of)
        den = saturate * (1.0 - length_slope + length_slope * length_of / average)
        dens.append(jnp.concatenate([den] * 4, axis=1))
    own_queries.wait()

    @pl.loop(0, 16)
    def _(i):
        @pl.when(not_me(i))
        def _():
            doc_from(i).wait_recv()

    pick_row = lax.broadcasted_iota(jnp.int32, (8, 16), 0)
    pick_col = lax.broadcasted_iota(jnp.int32, (8, 16), 1)
    pick = jnp.where(jnp.logical_and(pick_col == z * 4 + pick_row, pick_row < 3), 1.0, 0.0).astype(jnp.bfloat16)
    for b in range(8):
        cols = slice(b * 512, (b + 1) * 512)
        doc_out[:, cols] = jnp.dot(pick, doc_all[c, b], preferred_element_type=jnp.float32)
        for side in range(2):
            weight = doc_all[side, b].astype(jnp.float32)
            scaled = weight * (saturate + 1.0) / (weight + dens[side])
            masked[side * 16:side * 16 + 16, cols] = jnp.where(
                keep[side, :, cols] > 0.5, scaled, 0.0
            ).astype(jnp.bfloat16)

    part[...] = lax.dot_general(
        masked[...], query_rows[...], (((1,), (1,)), ((), ())), preferred_element_type=jnp.float32
    )
    for zp in range(4):
        for side in range(2):
            part_send[zp, side * 4:side * 4 + 4, :] = part[side * 16 + zp * 4:side * 16 + zp * 4 + 4, :]

    def part_to(i):
        return send(part_send.at[(v + i) % 4], part_all.at[v], part_s.at[i], part_r.at[v], ((v + i) % 4, d))

    def part_from(i):
        peer = (v + i) % 4
        return send(part_send.at[peer], part_all.at[peer], part_s.at[i], part_r.at[peer], (peer, d))

    for i in range(1, 4):
        part_to(i).start()
    part_all[v] = part_send[v]

    @pl.when(jnp.logical_not(straight))
    def _():
        for j in range(3):
            from_x(j).wait_send()

    for h in range(2):
        side_terms(h).wait_send()

    @pl.loop(0, 12)
    def _(m):
        @pl.when(jnp.logical_and(z < 3, m // 3 <= z))
        def _():
            go_up(m).wait_send()

        @pl.when(jnp.logical_and(z > 0, m // 3 >= z))
        def _():
            go_down(m).wait_send()

        go_y(m).wait_send()
        go_sibling(m, 0).wait_send()
        go_sibling(m, 1).wait_send()

    @pl.loop(1, 8)
    def _(i):
        meta_to(i).wait_send()

    @pl.loop(0, 16)
    def _(i):
        @pl.when(not_me(i))
        def _():
            doc_to(i).wait_send()

    for i in range(1, 4):
        part_from(i).wait_recv()
        part_to(i).wait_send()
    score_out[...] = (part_all[0] + part_all[1]) + (part_all[2] + part_all[3])


def local_kernel(hidden, w_vocab, lengths, query_terms, tile_routes):
    routes = jnp.pad(tile_routes[0].T.astype(jnp.float32), ((0, 0), (0, 96)))
    lens = jnp.broadcast_to(lengths.astype(jnp.float32)[:, None], (3, 128))
    meta = jnp.concatenate([routes, lens, jnp.zeros((1, 128), jnp.float32)], axis=0)
    width = hidden.shape[2]
    any_space, vmem = pl.BlockSpec(memory_space=pl.ANY), pl.BlockSpec(memory_space=pltpu.VMEM)
    dma = lambda count: pltpu.SemaphoreType.DMA((count,))
    docs, scores = pl.pallas_call(
        head_kernel,
        out_shape=(
            jax.ShapeDtypeStruct((8, 4096), jnp.float32),
            jax.ShapeDtypeStruct((8, 128), jnp.float32),
        ),
        in_specs=[any_space, any_space, any_space, vmem],
        out_specs=(vmem, vmem),
        scratch_shapes=[
            pltpu.VMEM((12, 256, width), jnp.bfloat16),
            pltpu.VMEM((4, CHUNK, width), jnp.bfloat16),
            pltpu.VMEM((128, 4096), jnp.bfloat16),
            pltpu.VMEM((8, 8, 128), jnp.float32),
            pltpu.VMEM((2, 16, 4096), jnp.float32),
            pltpu.VMEM((4, 16, CHUNK), jnp.float32),
            pltpu.VMEM((2, 16, 512), jnp.bfloat16),
            pltpu.VMEM((2, 8, 16, 512), jnp.bfloat16),
            pltpu.VMEM((32, 4096), jnp.bfloat16),
            pltpu.VMEM((32, 128), jnp.float32),
            pltpu.VMEM((4, 8, 128), jnp.float32),
            pltpu.VMEM((4, 8, 128), jnp.float32),
            dma(6), dma(3), dma(3), dma(2), dma(2), dma(12), dma(12), dma(12), dma(12), dma(12),
            dma(24), dma(24), dma(8), dma(8), dma(16), dma(16), dma(4), dma(4),
        ],
        compiler_params=pltpu.CompilerParams(
            collective_id=0, has_side_effects=True, vmem_limit_bytes=40 * 1024 * 1024
        ),
    )(hidden, w_vocab, query_terms, meta)
    doc_terms = docs[:3].astype(jnp.bfloat16)
    return doc_terms, scores.reshape(2, 4, 128)[:, :3].reshape(6, 128).T


def solution(mesh):
    shape = dict(mesh.shape)
    body = local_kernel if (shape["vocab"], shape["docs"]) == (4, 8) else local
    return jax.shard_map(
        body,
        mesh=mesh,
        in_specs=(
            P("docs", "vocab", None),
            P(("vocab", "docs"), None),
            P("docs"),
            P("docs", "vocab"),
            P("docs", "vocab", None),
        ),
        out_specs=(P("docs", "vocab"), P("docs", "vocab")),
        check_vma=False,
    )
```

```python
import jax
import jax.numpy as jnp
from jax import lax
from jax.experimental import pallas as pl
from jax.experimental.pallas import tpu as pltpu
from jax.sharding import PartitionSpec as P

saturate = 1.2
length_slope = 0.75


def pooled_rows(passage_rows, weights, lens_here):
    logits = lax.dot_general(
        passage_rows, weights, (((2,), (1,)), ((), ())), preferred_element_type=jnp.float32
    )
    places = lax.broadcasted_iota(jnp.int32, logits.shape, 1)
    activity = jnp.where(
        places < lens_here[:, None, None], jnp.log1p(jnp.maximum(logits, 0.0)), 0.0
    )
    return jnp.sum(activity, axis=1) / lens_here.astype(jnp.float32)[:, None]


def local(hidden, w_vocab, lengths, query_terms, tile_routes):
    members = lax.axis_size("docs")
    local_count = hidden.shape[0]
    lens_all = lax.all_gather(lengths, "docs", axis=0, tiled=True)
    passage_total = lens_all.shape[0]
    average = jnp.sum(lens_all.astype(jnp.float32)) / passage_total
    full_rows = lax.all_gather(hidden, "vocab", axis=1, tiled=True)
    doc_terms = pooled_rows(
        full_rows, lax.all_gather(w_vocab, "docs", axis=0, tiled=True), lengths
    ).astype(jnp.bfloat16)
    weight = doc_terms.astype(jnp.float32)
    denominator = saturate * (
        1.0 - length_slope + length_slope * lengths.astype(jnp.float32) / average
    )
    scaled = (weight * (saturate + 1.0) / (weight + denominator[:, None])).astype(jnp.bfloat16)
    term_count = scaled.shape[1]
    tile_count = term_count // 128
    my_routes = tile_routes[0]
    fanout = my_routes.shape[1]
    capacity = min(tile_count, max(4, 2 * tile_count * fanout // members))
    owners = lax.broadcasted_iota(jnp.int32, (1, 1, members), 2)
    is_listed = jnp.any(my_routes[:, :, None] == owners, axis=1)
    slot_index = jnp.cumsum(is_listed.astype(jnp.int32), axis=0) - 1
    slot_ids = lax.broadcasted_iota(jnp.int32, (1, capacity, 1), 1)
    selector = (is_listed.T[:, None, :] & (slot_index.T[:, None, :] == slot_ids)).astype(
        jnp.bfloat16
    )
    blocks = scaled.reshape(local_count, tile_count, 128)
    outgoing = jnp.einsum(
        "oct,ptk->ocpk", selector, blocks, preferred_element_type=jnp.float32
    ).astype(jnp.bfloat16)
    tile_ids = lax.broadcasted_iota(jnp.float32, (1, 1, tile_count), 2)
    labels = jnp.sum(selector.astype(jnp.float32) * tile_ids, axis=2).astype(jnp.bfloat16)
    arrived, labels_in = (
        lax.all_to_all(outgoing, "docs", split_axis=0, concat_axis=0, tiled=True),
        lax.all_to_all(labels, "docs", split_axis=0, concat_axis=0, tiled=True),
    )
    placing = (labels_in.astype(jnp.float32)[:, :, None] == tile_ids).astype(jnp.bfloat16)
    masked = jnp.einsum(
        "bct,bcpk->bptk", placing, arrived, preferred_element_type=jnp.float32
    ).astype(jnp.bfloat16)
    masked = masked.reshape(passage_total, term_count)
    partial_value = lax.dot_general(
        query_terms, masked, (((1,), (1,)), ((), ())), preferred_element_type=jnp.float32
    )
    scores = lax.psum_scatter(partial_value, "vocab", scatter_dimension=1, tiled=True)
    return (doc_terms, scores)


CHUNK = 256
MESH = pl.DeviceIdType.MESH


def head_kernel(
    hidden, weights, queries, meta, doc_out, score_out,
    rows, terms, query_rows, meta_all, keep, pooled, doc_send, doc_all, masked, part, part_send, part_all, sums_in,
    local_sem, w_s, w_r, up_s, down_s, z_r, y_s, y_r, sib_s, sib_r,
    meta_s, meta_r, doc_s, doc_r, part_s, part_r, sum_s, sum_r,
):
    v, d = lax.axis_index("vocab"), lax.axis_index("docs")
    x, y, z, c = v % 2, v // 2, d // 2, d % 2
    x_side, y_side = (2 * y + 1 - x, d), (2 * (1 - y) + x, d)
    sibling = (v, 2 * z + 1 - c)
    above, below = (v, d + 2), (v, d - 2)

    def send(src, dst, s_sem, r_sem, to):
        return pltpu.make_async_remote_copy(
            src_ref=src, dst_ref=dst, send_sem=s_sem, recv_sem=r_sem, device_id=to, device_id_type=MESH
        )

    barrier = pltpu.get_barrier_semaphore()

    @pl.loop(1, 8)
    def _(i):
        pl.semaphore_signal(barrier, inc=1, device_id=(v, (d + i) % 8), device_id_type=MESH)

    for i in range(1, 4):
        pl.semaphore_signal(barrier, inc=1, device_id=((v + i) % 4, d), device_id_type=MESH)
    pl.semaphore_wait(barrier, 10)

    def slot(m, vp):
        return rows.at[m, pl.ds(pl.multiple_of(vp * 64, 64), 64), :]

    def own_rows(j):
        return pltpu.make_async_copy(hidden.at[j], slot(z * 3 + j, 2 * c + y), local_sem.at[j])

    def own_terms(h):
        return pltpu.make_async_copy(
            weights.at[pl.ds(h * CHUNK, CHUNK), :], terms.at[x * 2 + h], local_sem.at[3 + h]
        )

    own_queries = pltpu.make_async_copy(queries, query_rows, local_sem.at[5])

    def side_terms(h):
        return send(weights.at[pl.ds(h * CHUNK, CHUNK), :], terms.at[x * 2 + h], w_s.at[h], w_r.at[h], x_side)

    def side_terms_in(h):
        return send(weights.at[pl.ds(h * CHUNK, CHUNK), :], terms.at[(1 - x) * 2 + h], w_s.at[h], w_r.at[h], x_side)

    def go_up(m):
        return send(slot(m, 2 * c + y), slot(m, 2 * c + y), up_s.at[m], z_r.at[m], above)

    def go_down(m):
        return send(slot(m, 2 * c + y), slot(m, 2 * c + y), down_s.at[m], z_r.at[m], below)

    def go_y(m):
        return send(slot(m, 2 * c + y), slot(m, 2 * c + y), y_s.at[m], y_r.at[m], y_side)

    def come_y(m):
        block = slot(m, 2 * c + 1 - y)
        return send(block, block, y_s.at[m], y_r.at[m], y_side)

    def go_sibling(m, side):
        block = slot(m, 2 * c + side)
        return send(block, block, sib_s.at[m * 2 + side], sib_r.at[m * 2 + side], sibling)

    def come_sibling(m, side):
        block = slot(m, 2 * (1 - c) + side)
        return send(block, block, sib_s.at[m * 2 + side], sib_r.at[m * 2 + side], sibling)

    for j in range(3):
        own_rows(j).start()
    for h in range(2):
        side_terms(h).start()

    def meta_to(i):
        peer = (d + i) % 8
        return send(meta, meta_all.at[d], meta_s.at[i], meta_r.at[d], (v, peer))

    def meta_from(i):
        peer = (d + i) % 8
        return send(meta, meta_all.at[peer], meta_s.at[i], meta_r.at[peer], (v, peer))

    @pl.loop(1, 8)
    def _(i):
        meta_to(i).start()

    meta_all[d] = meta[...]
    for h in range(2):
        own_terms(h).start()
    own_queries.start()
    pooled[...] = jnp.zeros_like(pooled)

    for j in range(3):
        own_rows(j).wait()
        m = z * 3 + j

        @pl.when(z < 3)
        def _():
            go_up(m).start()

        @pl.when(z > 0)
        def _():
            go_down(m).start()

        go_y(m).start()
        go_sibling(m, y).start()

    for h in range(2):
        own_terms(h).wait()

    @pl.loop(1, 8)
    def _(i):
        meta_from(i).wait_recv()

    row_id = lax.broadcasted_iota(jnp.int32, (16, 128), 0)
    mine = d.astype(jnp.float32)
    for side in range(2):
        listed = jnp.zeros((16, 128), jnp.float32)
        for zp in range(4):
            routes = meta_all[2 * zp + side][0:4, :]
            hit = jnp.max(jnp.where(routes == mine, 1.0, 0.0), axis=0, keepdims=True)
            listed = jnp.where(row_id // 4 == zp, hit, listed)
        for t in range(32):
            keep[side * 16:side * 16 + 16, t * 128:(t + 1) * 128] = jnp.broadcast_to(listed[:, t:t + 1], (16, 128))

    def order(n):
        end = jnp.logical_or(z == 0, z == 3)
        step = n - 3
        end_z = jnp.where(z == 0, z + step // 3 + 1, z - step // 3 - 1)
        near = jnp.where(step % 2 == 0, z - 1, z + 1)
        mid_z = jnp.where(n < 9, near, jnp.where(z == 1, 3, 0))
        mid_j = jnp.where(n < 9, step // 2, n - 9)
        zp = jnp.where(n < 3, z, jnp.where(end, end_z, mid_z))
        j = jnp.where(n < 3, n, jnp.where(end, step % 3, mid_j))
        return zp, j

    place = lax.broadcasted_iota(jnp.int32, (8, CHUNK), 0).astype(jnp.float32)

    def pool(n, q):
        zp, j = order(n)
        m = zp * 3 + j
        logits = lax.dot_general(
            rows[m], terms[q], (((1,), (1,)), ((), ())), preferred_element_type=jnp.float32
        )
        for core in range(2):
            length = meta_all[2 * zp + core, pl.ds(4 + j, 1), :]
            length = jnp.concatenate([length] * (CHUNK // 128), axis=1)
            total = jnp.zeros((8, CHUNK), jnp.float32)
            for side in range(2):
                room = length - place - (64 * x + 128 * side).astype(jnp.float32)
                at = 128 * core + 64 * side
                parts = [
                    jnp.where(room > float(8 * i), jnp.maximum(logits[at + 8 * i:at + 8 * i + 8, :], 0.0), 0.0)
                    for i in range(8)
                ]
                while len(parts) > 1:
                    parts = [a + b + a * b for a, b in zip(parts[0::2], parts[1::2])]
                total = total + jnp.log1p(parts[0])
            pooled[q, pl.ds(core * 16 + zp * 4 + j, 1), :] = jnp.sum(total, axis=0, keepdims=True)

    def sums_to(h):
        return send(pooled.at[(1 - x) * 2 + h], sums_in.at[h], sum_s.at[h], sum_r.at[h], x_side)

    @pl.loop(0, 12)
    def _(n):
        k, j = n // 3 + 1, n % 3

        @pl.when(jnp.logical_and(n < 9, z - k >= 0))
        def _():
            m = (z - k) * 3 + j
            go_up(m).wait_recv()

            @pl.when(z < 3)
            def _():
                go_up(m).start()

            go_y(m).start()
            go_sibling(m, y).start()

        @pl.when(jnp.logical_and(n < 9, z + k <= 3))
        def _():
            m = (z + k) * 3 + j
            go_down(m).wait_recv()

            @pl.when(z > 0)
            def _():
                go_down(m).start()

            go_y(m).start()
            go_sibling(m, y).start()

        zp, jj = order(n)
        m = zp * 3 + jj
        come_y(m).wait_recv()
        go_sibling(m, 1 - y).start()

        come_sibling(m, 0).wait_recv()
        come_sibling(m, 1).wait_recv()

        for h, first in ((0, 5), (1, 9)):
            @pl.when(n == first)
            def _():
                side_terms_in(h).wait_recv()

        @pl.loop(0, 4)
        def _(i):
            first = jnp.where(i == 0, 5, jnp.where(i == 1, 9, 0))
            start = jnp.where(n == first, 0, n)
            stop = jnp.where(n >= first, n + 1, start)
            q = jnp.where(i < 2, (1 - x) * 2 + i, x * 2 + i - 2)

            def step(at, carry):
                pool(at, q)
                return carry

            lax.fori_loop(start, stop, step, 0)

            @pl.when(jnp.logical_and(n == 11, i < 2))
            def _():
                sums_to(i).start()

    row_32 = lax.broadcasted_iota(jnp.int32, (32, 128), 0)
    length_of = jnp.ones((32, 128), jnp.float32)
    for b in range(8):
        for j in range(3):
            length_of = jnp.where(row_32 == b % 2 * 16 + b // 2 * 4 + j, meta_all[b, 4 + j:5 + j, :], length_of)
    length_wide = jnp.concatenate([length_of] * (CHUNK // 128), axis=1)
    for h in range(2):
        sums_to(h).wait_recv()
        total = pooled[x * 2 + h] + sums_in[h]
        doc_send[:, h * CHUNK:(h + 1) * CHUNK] = (total / length_wide).astype(jnp.bfloat16)

    def doc_to(i):
        return send(doc_send, doc_all.at[d], doc_s.at[i], doc_r.at[d], (v, (d + i) % 8))

    def doc_from(i):
        peer = (d + i) % 8
        return send(doc_send, doc_all.at[peer], doc_s.at[i], doc_r.at[peer], (v, peer))

    @pl.loop(1, 8)
    def _(i):
        doc_to(i).start()

    doc_all[d] = doc_send[...]

    length_sum = jnp.zeros((1, 128), jnp.float32)
    for b in range(8):
        for j in range(3):
            length_sum = length_sum + meta_all[b, 4 + j:5 + j, :]
    average = length_sum / 24.0
    den = saturate * (1.0 - length_slope + length_slope * length_of / average)
    den = jnp.concatenate([den] * 4, axis=1)
    own_queries.wait()

    @pl.loop(1, 8)
    def _(i):
        doc_from(i).wait_recv()

    pick_row = lax.broadcasted_iota(jnp.int32, (8, 32), 0)
    pick_col = lax.broadcasted_iota(jnp.int32, (8, 32), 1)
    pick = jnp.logical_and(pick_col == c * 16 + z * 4 + pick_row, pick_row < 3)
    pick = jnp.where(pick, 1.0, 0.0).astype(jnp.bfloat16)
    for b in range(8):
        cols = slice(b * 512, (b + 1) * 512)
        doc_out[:, cols] = jnp.dot(pick, doc_all[b], preferred_element_type=jnp.float32)
        weight = doc_all[b].astype(jnp.float32)
        scaled = weight * (saturate + 1.0) / (weight + den)
        masked[:, cols] = jnp.where(keep[:, cols] > 0.5, scaled, 0.0).astype(jnp.bfloat16)

    part[...] = lax.dot_general(
        masked[...], query_rows[...], (((1,), (1,)), ((), ())), preferred_element_type=jnp.float32
    )
    for zp in range(4):
        for side in range(2):
            part_send[zp, side * 4:side * 4 + 4, :] = part[side * 16 + zp * 4:side * 16 + zp * 4 + 4, :]

    def part_to(i):
        return send(part_send.at[(v + i) % 4], part_all.at[v], part_s.at[i], part_r.at[v], ((v + i) % 4, d))

    def part_from(i):
        peer = (v + i) % 4
        return send(part_send.at[peer], part_all.at[peer], part_s.at[i], part_r.at[peer], (peer, d))

    for i in range(1, 4):
        part_to(i).start()
    part_all[v] = part_send[v]

    for h in range(2):
        side_terms(h).wait_send()
        sums_to(h).wait_send()

    @pl.loop(0, 12)
    def _(m):
        @pl.when(jnp.logical_and(z < 3, m // 3 <= z))
        def _():
            go_up(m).wait_send()

        @pl.when(jnp.logical_and(z > 0, m // 3 >= z))
        def _():
            go_down(m).wait_send()

        go_y(m).wait_send()
        go_sibling(m, 0).wait_send()
        go_sibling(m, 1).wait_send()

    @pl.loop(1, 8)
    def _(i):
        meta_to(i).wait_send()

    @pl.loop(1, 8)
    def _(i):
        doc_to(i).wait_send()

    for i in range(1, 4):
        part_from(i).wait_recv()
        part_to(i).wait_send()
    score_out[...] = (part_all[0] + part_all[1]) + (part_all[2] + part_all[3])


def local_kernel(hidden, w_vocab, lengths, query_terms, tile_routes):
    routes = jnp.pad(tile_routes[0].T.astype(jnp.float32), ((0, 0), (0, 96)))
    lens = jnp.broadcast_to(lengths.astype(jnp.float32)[:, None], (3, 128))
    meta = jnp.concatenate([routes, lens, jnp.zeros((1, 128), jnp.float32)], axis=0)
    width = hidden.shape[2]
    any_space, vmem = pl.BlockSpec(memory_space=pl.ANY), pl.BlockSpec(memory_space=pltpu.VMEM)
    dma = lambda count: pltpu.SemaphoreType.DMA((count,))
    docs, scores = pl.pallas_call(
        head_kernel,
        out_shape=(
            jax.ShapeDtypeStruct((8, 4096), jnp.float32),
            jax.ShapeDtypeStruct((8, 128), jnp.float32),
        ),
        in_specs=[any_space, any_space, any_space, vmem],
        out_specs=(vmem, vmem),
        scratch_shapes=[
            pltpu.VMEM((12, 256, width), jnp.bfloat16),
            pltpu.VMEM((4, CHUNK, width), jnp.bfloat16),
            pltpu.VMEM((128, 4096), jnp.bfloat16),
            pltpu.VMEM((8, 8, 128), jnp.float32),
            pltpu.VMEM((32, 4096), jnp.float32),
            pltpu.VMEM((4, 32, CHUNK), jnp.float32),
            pltpu.VMEM((32, 512), jnp.bfloat16),
            pltpu.VMEM((8, 32, 512), jnp.bfloat16),
            pltpu.VMEM((32, 4096), jnp.bfloat16),
            pltpu.VMEM((32, 128), jnp.float32),
            pltpu.VMEM((4, 8, 128), jnp.float32),
            pltpu.VMEM((4, 8, 128), jnp.float32),
            pltpu.VMEM((2, 32, CHUNK), jnp.float32),
            dma(6), dma(2), dma(2), dma(12), dma(12), dma(12), dma(12), dma(12), dma(24), dma(24),
            dma(8), dma(8), dma(8), dma(8), dma(4), dma(4), dma(2), dma(2),
        ],
        compiler_params=pltpu.CompilerParams(
            collective_id=0, has_side_effects=True, vmem_limit_bytes=60 * 1024 * 1024
        ),
    )(hidden, w_vocab, query_terms, meta)
    doc_terms = docs[:3].astype(jnp.bfloat16)
    return doc_terms, scores.reshape(2, 4, 128)[:, :3].reshape(6, 128).T


def solution(mesh):
    shape = dict(mesh.shape)
    body = local_kernel if (shape["vocab"], shape["docs"]) == (4, 8) else local
    return jax.shard_map(
        body,
        mesh=mesh,
        in_specs=(
            P("docs", "vocab", None),
            P(("vocab", "docs"), None),
            P("docs"),
            P("docs", "vocab"),
            P("docs", "vocab", None),
        ),
        out_specs=(P("docs", "vocab"), P("docs", "vocab")),
        check_vma=False,
    )
```

```python
import jax
import jax.numpy as jnp
from jax import lax
from jax.experimental import pallas as pl
from jax.experimental.pallas import tpu as pltpu
from jax.sharding import PartitionSpec as P

saturate = 1.2
length_slope = 0.75


def pooled_rows(passage_rows, weights, lens_here):
    logits = lax.dot_general(
        passage_rows, weights, (((2,), (1,)), ((), ())), preferred_element_type=jnp.float32
    )
    places = lax.broadcasted_iota(jnp.int32, logits.shape, 1)
    activity = jnp.where(
        places < lens_here[:, None, None], jnp.log1p(jnp.maximum(logits, 0.0)), 0.0
    )
    return jnp.sum(activity, axis=1) / lens_here.astype(jnp.float32)[:, None]


def local(hidden, w_vocab, lengths, query_terms, tile_routes):
    members = lax.axis_size("docs")
    local_count = hidden.shape[0]
    lens_all = lax.all_gather(lengths, "docs", axis=0, tiled=True)
    passage_total = lens_all.shape[0]
    average = jnp.sum(lens_all.astype(jnp.float32)) / passage_total
    full_rows = lax.all_gather(hidden, "vocab", axis=1, tiled=True)
    doc_terms = pooled_rows(
        full_rows, lax.all_gather(w_vocab, "docs", axis=0, tiled=True), lengths
    ).astype(jnp.bfloat16)
    weight = doc_terms.astype(jnp.float32)
    denominator = saturate * (
        1.0 - length_slope + length_slope * lengths.astype(jnp.float32) / average
    )
    scaled = (weight * (saturate + 1.0) / (weight + denominator[:, None])).astype(jnp.bfloat16)
    term_count = scaled.shape[1]
    tile_count = term_count // 128
    my_routes = tile_routes[0]
    fanout = my_routes.shape[1]
    capacity = min(tile_count, max(4, 2 * tile_count * fanout // members))
    owners = lax.broadcasted_iota(jnp.int32, (1, 1, members), 2)
    is_listed = jnp.any(my_routes[:, :, None] == owners, axis=1)
    slot_index = jnp.cumsum(is_listed.astype(jnp.int32), axis=0) - 1
    slot_ids = lax.broadcasted_iota(jnp.int32, (1, capacity, 1), 1)
    selector = (is_listed.T[:, None, :] & (slot_index.T[:, None, :] == slot_ids)).astype(
        jnp.bfloat16
    )
    blocks = scaled.reshape(local_count, tile_count, 128)
    outgoing = jnp.einsum(
        "oct,ptk->ocpk", selector, blocks, preferred_element_type=jnp.float32
    ).astype(jnp.bfloat16)
    tile_ids = lax.broadcasted_iota(jnp.float32, (1, 1, tile_count), 2)
    labels = jnp.sum(selector.astype(jnp.float32) * tile_ids, axis=2).astype(jnp.bfloat16)
    arrived, labels_in = (
        lax.all_to_all(outgoing, "docs", split_axis=0, concat_axis=0, tiled=True),
        lax.all_to_all(labels, "docs", split_axis=0, concat_axis=0, tiled=True),
    )
    placing = (labels_in.astype(jnp.float32)[:, :, None] == tile_ids).astype(jnp.bfloat16)
    masked = jnp.einsum(
        "bct,bcpk->bptk", placing, arrived, preferred_element_type=jnp.float32
    ).astype(jnp.bfloat16)
    masked = masked.reshape(passage_total, term_count)
    partial_value = lax.dot_general(
        query_terms, masked, (((1,), (1,)), ((), ())), preferred_element_type=jnp.float32
    )
    scores = lax.psum_scatter(partial_value, "vocab", scatter_dimension=1, tiled=True)
    return (doc_terms, scores)


CHUNK = 256
MESH = pl.DeviceIdType.MESH


def head_kernel(
    hidden, weights, queries, meta, doc_out, score_out,
    rows, terms, turned, query_rows, meta_all, keep, pooled, doc_send, doc_all, masked, part, part_send, part_all, sums_in,
    local_sem, w_s, w_r, up_s, down_s, z_r, y_s, y_r, sib_s, sib_r,
    meta_s, meta_r, doc_s, doc_r, part_s, part_r, sum_s, sum_r,
):
    v, d = lax.axis_index("vocab"), lax.axis_index("docs")
    x, y, z, c = v % 2, v // 2, d // 2, d % 2
    x_side, y_side = (2 * y + 1 - x, d), (2 * (1 - y) + x, d)
    sibling = (v, 2 * z + 1 - c)
    above, below = (v, d + 2), (v, d - 2)

    def send(src, dst, s_sem, r_sem, to):
        return pltpu.make_async_remote_copy(
            src_ref=src, dst_ref=dst, send_sem=s_sem, recv_sem=r_sem, device_id=to, device_id_type=MESH
        )

    barrier = pltpu.get_barrier_semaphore()

    @pl.loop(1, 8)
    def _(i):
        pl.semaphore_signal(barrier, inc=1, device_id=(v, (d + i) % 8), device_id_type=MESH)

    for i in range(1, 4):
        pl.semaphore_signal(barrier, inc=1, device_id=((v + i) % 4, d), device_id_type=MESH)
    pl.semaphore_wait(barrier, 10)

    def slot(m, vp):
        return rows.at[m, pl.ds(pl.multiple_of(vp * 64, 64), 64), :]

    def own_rows(j):
        return pltpu.make_async_copy(hidden.at[j], slot(z * 3 + j, 2 * c + y), local_sem.at[j])

    def own_terms(h):
        return pltpu.make_async_copy(
            weights.at[pl.ds(h * CHUNK, CHUNK), :], terms.at[x * 2 + h], local_sem.at[3 + h]
        )

    own_queries = pltpu.make_async_copy(queries, query_rows, local_sem.at[5])

    def side_terms(h):
        return send(weights.at[pl.ds(h * CHUNK, CHUNK), :], terms.at[x * 2 + h], w_s.at[h], w_r.at[h], x_side)

    def side_terms_in(h):
        return send(weights.at[pl.ds(h * CHUNK, CHUNK), :], terms.at[(1 - x) * 2 + h], w_s.at[h], w_r.at[h], x_side)

    def go_up(m, side):
        block, at = slot(m, 2 * c + side), m * 2 + side
        return send(block, block, up_s.at[at], z_r.at[at], above)

    def go_down(m, side):
        block, at = slot(m, 2 * c + side), m * 2 + side
        return send(block, block, down_s.at[at], z_r.at[at], below)

    def onward(m, side, up, down):
        @pl.when(jnp.logical_and(up, z < 3))
        def _():
            go_up(m, side).start()

        @pl.when(jnp.logical_and(down, z > 0))
        def _():
            go_down(m, side).start()

    def y_first(j):
        return jnp.logical_and(c == 0, j == 0)

    def go_y(m):
        return send(slot(m, 2 * c + y), slot(m, 2 * c + y), y_s.at[m], y_r.at[m], y_side)

    def come_y(m):
        block = slot(m, 2 * c + 1 - y)
        return send(block, block, y_s.at[m], y_r.at[m], y_side)

    def go_sibling(m, side):
        block = slot(m, 2 * c + side)
        return send(block, block, sib_s.at[m * 2 + side], sib_r.at[m * 2 + side], sibling)

    def come_sibling(m, side):
        block = slot(m, 2 * (1 - c) + side)
        return send(block, block, sib_s.at[m * 2 + side], sib_r.at[m * 2 + side], sibling)

    for j in range(3):
        own_rows(j).start()
    for h in range(2):
        side_terms(h).start()

    def meta_to(i):
        peer = (d + i) % 8
        return send(meta, meta_all.at[d], meta_s.at[i], meta_r.at[d], (v, peer))

    def meta_from(i):
        peer = (d + i) % 8
        return send(meta, meta_all.at[peer], meta_s.at[i], meta_r.at[peer], (v, peer))

    @pl.loop(1, 8)
    def _(i):
        meta_to(i).start()

    meta_all[d] = meta[...]
    for h in range(2):
        own_terms(h).start()
    own_queries.start()
    pooled[...] = jnp.zeros_like(pooled)

    for j in range(3):
        own_rows(j).wait()
        m = z * 3 + j

        onward(m, y, True, True)
        go_y(m).start()
        go_sibling(m, y).start()

    for h in range(2):
        own_terms(h).wait()
        turned[x * 2 + h] = terms[x * 2 + h].T

    @pl.loop(1, 8)
    def _(i):
        meta_from(i).wait_recv()

    row_id = lax.broadcasted_iota(jnp.int32, (16, 128), 0)
    mine = d.astype(jnp.float32)
    for side in range(2):
        listed = jnp.zeros((16, 128), jnp.float32)
        for zp in range(4):
            routes = meta_all[2 * zp + side][0:4, :]
            hit = jnp.max(jnp.where(routes == mine, 1.0, 0.0), axis=0, keepdims=True)
            listed = jnp.where(row_id // 4 == zp, hit, listed)
        for t in range(32):
            keep[side * 16:side * 16 + 16, t * 128:(t + 1) * 128] = jnp.broadcast_to(listed[:, t:t + 1], (16, 128))

    def order(n):
        end = jnp.logical_or(z == 0, z == 3)
        step = n - 3
        end_z = jnp.where(z == 0, z + step // 3 + 1, z - step // 3 - 1)
        near = jnp.where(step % 2 == 0, z - 1, z + 1)
        mid_z = jnp.where(n < 9, near, jnp.where(z == 1, 3, 0))
        mid_j = jnp.where(n < 9, step // 2, n - 9)
        zp = jnp.where(n < 3, z, jnp.where(end, end_z, mid_z))
        j = jnp.where(n < 3, n, jnp.where(end, step % 3, mid_j))
        return zp, j

    place = lax.broadcasted_iota(jnp.int32, (8, CHUNK), 0).astype(jnp.float32)

    def pool(n, q):
        zp, j = order(n)
        m = zp * 3 + j
        logits = lax.dot_general(
            rows[m], turned[q], (((1,), (0,)), ((), ())), preferred_element_type=jnp.float32
        )
        for core in range(2):
            length = meta_all[2 * zp + core, pl.ds(4 + j, 1), :]
            length = jnp.concatenate([length] * (CHUNK // 128), axis=1)
            total = jnp.zeros((8, CHUNK), jnp.float32)
            for side in range(2):
                room = length - place - (64 * x + 128 * side).astype(jnp.float32)
                at = 128 * core + 64 * side
                parts = [
                    jnp.where(room > float(8 * i), jnp.maximum(logits[at + 8 * i:at + 8 * i + 8, :], 0.0), 0.0)
                    for i in range(8)
                ]
                while len(parts) > 1:
                    parts = [a + b + a * b for a, b in zip(parts[0::2], parts[1::2])]
                total = total + jnp.log1p(parts[0])
            pooled[q, pl.ds(core * 16 + zp * 4 + j, 1), :] = jnp.sum(total, axis=0, keepdims=True)

    def sums_to(h):
        return send(pooled.at[(1 - x) * 2 + h], sums_in.at[h], sum_s.at[h], sum_r.at[h], x_side)

    def from_z(zp, j, up):
        m = zp * 3 + j
        go_up(m, y).wait_recv()
        onward(m, y, up, not up)

        @pl.when(jnp.logical_not(y_first(j)))
        def _():
            go_y(m).start()

        go_sibling(m, y).start()

        @pl.when(jnp.logical_and(c == 0, j == 2))
        def _():
            first = zp * 3
            go_up(first, 1 - y).wait_recv()
            onward(first, 1 - y, up, not up)
            go_sibling(first, 1 - y).start()

    @pl.loop(0, 12)
    def _(n):
        zp, jj = order(n)
        m = zp * 3 + jj

        @pl.when(jnp.logical_or(jnp.logical_not(y_first(jj)), zp == z))
        def _():
            come_y(m).wait_recv()

            @pl.when(y_first(jj))
            def _():
                onward(m, 1 - y, True, True)

            go_sibling(m, 1 - y).start()

        k, j = n // 3 + 1, n % 3

        @pl.when(jnp.logical_and(n < 9, z - k >= 0))
        def _():
            from_z(z - k, j, True)

        @pl.when(jnp.logical_and(n < 9, z + k <= 3))
        def _():
            from_z(z + k, j, False)

        come_sibling(m, 0).wait_recv()
        come_sibling(m, 1).wait_recv()

        for h, first in ((0, 5), (1, 8)):
            @pl.when(n == first)
            def _():
                side_terms_in(h).wait_recv()
                turned[(1 - x) * 2 + h] = terms[(1 - x) * 2 + h].T

        @pl.loop(0, 4)
        def _(i):
            late = 4 * (n - 8) - (n - 8) // 3
            start = jnp.where(i == 1, jnp.where(n < 8, n, late), jnp.where(jnp.logical_and(i == 0, n == 5), 0, n))
            late_stop = jnp.where(n < 8, n, jnp.minimum(4 * (n - 7) - (n - 7) // 3, 12))
            early_stop = jnp.where(jnp.logical_and(i == 0, n < 5), n, n + 1)
            stop = jnp.where(i == 1, late_stop, early_stop)
            q = jnp.where(i < 2, (1 - x) * 2 + i, x * 2 + i - 2)

            def step(at, carry):
                pool(at, q)
                return carry

            lax.fori_loop(start, stop, step, 0)

            @pl.when(jnp.logical_and(n == 11, i < 2))
            def _():
                sums_to(i).start()

    row_32 = lax.broadcasted_iota(jnp.int32, (32, 128), 0)
    length_of = jnp.ones((32, 128), jnp.float32)
    for b in range(8):
        for j in range(3):
            length_of = jnp.where(row_32 == b % 2 * 16 + b // 2 * 4 + j, meta_all[b, 4 + j:5 + j, :], length_of)
    length_wide = jnp.concatenate([length_of] * (CHUNK // 128), axis=1)
    for h in range(2):
        sums_to(h).wait_recv()
        total = pooled[x * 2 + h] + sums_in[h]
        doc_send[:, h * CHUNK:(h + 1) * CHUNK] = (total / length_wide).astype(jnp.bfloat16)

    def doc_to(i):
        return send(doc_send, doc_all.at[d], doc_s.at[i], doc_r.at[d], (v, (d + i) % 8))

    def doc_from(i):
        peer = (d + i) % 8
        return send(doc_send, doc_all.at[peer], doc_s.at[i], doc_r.at[peer], (v, peer))

    @pl.loop(1, 8)
    def _(i):
        doc_to(i).start()

    doc_all[d] = doc_send[...]

    length_sum = jnp.zeros((1, 128), jnp.float32)
    for b in range(8):
        for j in range(3):
            length_sum = length_sum + meta_all[b, 4 + j:5 + j, :]
    average = length_sum / 24.0
    den = saturate * (1.0 - length_slope + length_slope * length_of / average)
    den = jnp.concatenate([den] * 4, axis=1)
    own_queries.wait()

    @pl.loop(1, 8)
    def _(i):
        doc_from(i).wait_recv()

    pick_row = lax.broadcasted_iota(jnp.int32, (8, 32), 0)
    pick_col = lax.broadcasted_iota(jnp.int32, (8, 32), 1)
    pick = jnp.logical_and(pick_col == c * 16 + z * 4 + pick_row, pick_row < 3)
    pick = jnp.where(pick, 1.0, 0.0).astype(jnp.bfloat16)
    for b in range(8):
        cols = slice(b * 512, (b + 1) * 512)
        doc_out[:, cols] = jnp.dot(pick, doc_all[b], preferred_element_type=jnp.float32)
        weight = doc_all[b].astype(jnp.float32)
        scaled = weight * (saturate + 1.0) / (weight + den)
        masked[:, cols] = jnp.where(keep[:, cols] > 0.5, scaled, 0.0).astype(jnp.bfloat16)

    part[...] = lax.dot_general(
        masked[...], query_rows[...], (((1,), (1,)), ((), ())), preferred_element_type=jnp.float32
    )
    for zp in range(4):
        for side in range(2):
            part_send[zp, side * 4:side * 4 + 4, :] = part[side * 16 + zp * 4:side * 16 + zp * 4 + 4, :]

    def part_to(i):
        return send(part_send.at[(v + i) % 4], part_all.at[v], part_s.at[i], part_r.at[v], ((v + i) % 4, d))

    def part_from(i):
        peer = (v + i) % 4
        return send(part_send.at[peer], part_all.at[peer], part_s.at[i], part_r.at[peer], (peer, d))

    for i in range(1, 4):
        part_to(i).start()
    part_all[v] = part_send[v]

    for h in range(2):
        side_terms(h).wait_send()
        sums_to(h).wait_send()

    @pl.loop(0, 12)
    def _(m):
        zp, j = m // 3, m % 3
        crossed = jnp.logical_and(y_first(j), zp != z)
        for side, there in ((y, True), (1 - y, y_first(j))):
            @pl.when(jnp.logical_and(there, jnp.logical_and(z < 3, zp <= z)))
            def _():
                go_up(m, side).wait_send()

            @pl.when(jnp.logical_and(there, jnp.logical_and(z > 0, zp >= z)))
            def _():
                go_down(m, side).wait_send()

        @pl.when(jnp.logical_not(crossed))
        def _():
            go_y(m).wait_send()

        go_sibling(m, 0).wait_send()
        go_sibling(m, 1).wait_send()

    @pl.loop(1, 8)
    def _(i):
        meta_to(i).wait_send()

    @pl.loop(1, 8)
    def _(i):
        doc_to(i).wait_send()

    for i in range(1, 4):
        part_from(i).wait_recv()
        part_to(i).wait_send()
    score_out[...] = (part_all[0] + part_all[1]) + (part_all[2] + part_all[3])


def local_kernel(hidden, w_vocab, lengths, query_terms, tile_routes):
    routes = jnp.pad(tile_routes[0].T.astype(jnp.float32), ((0, 0), (0, 96)))
    lens = jnp.broadcast_to(lengths.astype(jnp.float32)[:, None], (3, 128))
    meta = jnp.concatenate([routes, lens, jnp.zeros((1, 128), jnp.float32)], axis=0)
    width = hidden.shape[2]
    any_space, vmem = pl.BlockSpec(memory_space=pl.ANY), pl.BlockSpec(memory_space=pltpu.VMEM)
    dma = lambda count: pltpu.SemaphoreType.DMA((count,))
    docs, scores = pl.pallas_call(
        head_kernel,
        out_shape=(
            jax.ShapeDtypeStruct((8, 4096), jnp.float32),
            jax.ShapeDtypeStruct((8, 128), jnp.float32),
        ),
        in_specs=[any_space, any_space, any_space, vmem],
        out_specs=(vmem, vmem),
        scratch_shapes=[
            pltpu.VMEM((12, 256, width), jnp.bfloat16),
            pltpu.VMEM((4, CHUNK, width), jnp.bfloat16),
            pltpu.VMEM((4, width, CHUNK), jnp.bfloat16),
            pltpu.VMEM((128, 4096), jnp.bfloat16),
            pltpu.VMEM((8, 8, 128), jnp.float32),
            pltpu.VMEM((32, 4096), jnp.float32),
            pltpu.VMEM((4, 32, CHUNK), jnp.float32),
            pltpu.VMEM((32, 512), jnp.bfloat16),
            pltpu.VMEM((8, 32, 512), jnp.bfloat16),
            pltpu.VMEM((32, 4096), jnp.bfloat16),
            pltpu.VMEM((32, 128), jnp.float32),
            pltpu.VMEM((4, 8, 128), jnp.float32),
            pltpu.VMEM((4, 8, 128), jnp.float32),
            pltpu.VMEM((2, 32, CHUNK), jnp.float32),
            dma(6), dma(2), dma(2), dma(24), dma(24), dma(24), dma(12), dma(12), dma(24), dma(24),
            dma(8), dma(8), dma(8), dma(8), dma(4), dma(4), dma(2), dma(2),
        ],
        compiler_params=pltpu.CompilerParams(
            collective_id=0, has_side_effects=True, vmem_limit_bytes=60 * 1024 * 1024
        ),
    )(hidden, w_vocab, query_terms, meta)
    doc_terms = docs[:3].astype(jnp.bfloat16)
    return doc_terms, scores.reshape(2, 4, 128)[:, :3].reshape(6, 128).T


def solution(mesh):
    shape = dict(mesh.shape)
    body = local_kernel if (shape["vocab"], shape["docs"]) == (4, 8) else local
    return jax.shard_map(
        body,
        mesh=mesh,
        in_specs=(
            P("docs", "vocab", None),
            P(("vocab", "docs"), None),
            P("docs"),
            P("docs", "vocab"),
            P("docs", "vocab", None),
        ),
        out_specs=(P("docs", "vocab"), P("docs", "vocab")),
        check_vma=False,
    )
```

```python
import jax
import jax.numpy as jnp
from jax import lax
from jax.experimental import pallas as pl
from jax.experimental.pallas import tpu as pltpu
from jax.sharding import PartitionSpec as P

saturate = 1.2
length_slope = 0.75


def pooled_rows(passage_rows, weights, lens_here):
    logits = lax.dot_general(
        passage_rows, weights, (((2,), (1,)), ((), ())), preferred_element_type=jnp.float32
    )
    places = lax.broadcasted_iota(jnp.int32, logits.shape, 1)
    activity = jnp.where(
        places < lens_here[:, None, None], jnp.log1p(jnp.maximum(logits, 0.0)), 0.0
    )
    return jnp.sum(activity, axis=1) / lens_here.astype(jnp.float32)[:, None]


def local(hidden, w_vocab, lengths, query_terms, tile_routes):
    members = lax.axis_size("docs")
    local_count = hidden.shape[0]
    lens_all = lax.all_gather(lengths, "docs", axis=0, tiled=True)
    passage_total = lens_all.shape[0]
    average = jnp.sum(lens_all.astype(jnp.float32)) / passage_total
    full_rows = lax.all_gather(hidden, "vocab", axis=1, tiled=True)
    doc_terms = pooled_rows(
        full_rows, lax.all_gather(w_vocab, "docs", axis=0, tiled=True), lengths
    ).astype(jnp.bfloat16)
    weight = doc_terms.astype(jnp.float32)
    denominator = saturate * (
        1.0 - length_slope + length_slope * lengths.astype(jnp.float32) / average
    )
    scaled = (weight * (saturate + 1.0) / (weight + denominator[:, None])).astype(jnp.bfloat16)
    term_count = scaled.shape[1]
    tile_count = term_count // 128
    my_routes = tile_routes[0]
    fanout = my_routes.shape[1]
    capacity = min(tile_count, max(4, 2 * tile_count * fanout // members))
    owners = lax.broadcasted_iota(jnp.int32, (1, 1, members), 2)
    is_listed = jnp.any(my_routes[:, :, None] == owners, axis=1)
    slot_index = jnp.cumsum(is_listed.astype(jnp.int32), axis=0) - 1
    slot_ids = lax.broadcasted_iota(jnp.int32, (1, capacity, 1), 1)
    selector = (is_listed.T[:, None, :] & (slot_index.T[:, None, :] == slot_ids)).astype(
        jnp.bfloat16
    )
    blocks = scaled.reshape(local_count, tile_count, 128)
    outgoing = jnp.einsum(
        "oct,ptk->ocpk", selector, blocks, preferred_element_type=jnp.float32
    ).astype(jnp.bfloat16)
    tile_ids = lax.broadcasted_iota(jnp.float32, (1, 1, tile_count), 2)
    labels = jnp.sum(selector.astype(jnp.float32) * tile_ids, axis=2).astype(jnp.bfloat16)
    arrived, labels_in = (
        lax.all_to_all(outgoing, "docs", split_axis=0, concat_axis=0, tiled=True),
        lax.all_to_all(labels, "docs", split_axis=0, concat_axis=0, tiled=True),
    )
    placing = (labels_in.astype(jnp.float32)[:, :, None] == tile_ids).astype(jnp.bfloat16)
    masked = jnp.einsum(
        "bct,bcpk->bptk", placing, arrived, preferred_element_type=jnp.float32
    ).astype(jnp.bfloat16)
    masked = masked.reshape(passage_total, term_count)
    partial_value = lax.dot_general(
        query_terms, masked, (((1,), (1,)), ((), ())), preferred_element_type=jnp.float32
    )
    scores = lax.psum_scatter(partial_value, "vocab", scatter_dimension=1, tiled=True)
    return (doc_terms, scores)


CHUNK = 256
MESH = pl.DeviceIdType.MESH


def head_kernel(
    hidden, weights, queries, meta, doc_out, score_out,
    rows, terms, turned, query_rows, meta_all, keep, pooled, doc_send, doc_all, masked, part, part_send, part_all, sums_in,
    local_sem, w_s, w_r, up_s, down_s, z_r, y_s, y_r, sib_s, sib_r,
    meta_s, meta_r, doc_s, doc_r, part_s, part_r, sum_s, sum_r,
):
    v, d = lax.axis_index("vocab"), lax.axis_index("docs")
    x, y, z, c = v % 2, v // 2, d // 2, d % 2
    x_side, y_side = (2 * y + 1 - x, d), (2 * (1 - y) + x, d)
    sibling = (v, 2 * z + 1 - c)
    above, below = (v, d + 2), (v, d - 2)

    def send(src, dst, s_sem, r_sem, to):
        return pltpu.make_async_remote_copy(
            src_ref=src, dst_ref=dst, send_sem=s_sem, recv_sem=r_sem, device_id=to, device_id_type=MESH
        )

    barrier = pltpu.get_barrier_semaphore()

    @pl.loop(1, 8)
    def _(i):
        pl.semaphore_signal(barrier, inc=1, device_id=(v, (d + i) % 8), device_id_type=MESH)

    for i in range(1, 4):
        pl.semaphore_signal(barrier, inc=1, device_id=((v + i) % 4, d), device_id_type=MESH)
    pl.semaphore_wait(barrier, 10)

    def slot(m, vp):
        return rows.at[m, pl.ds(pl.multiple_of(vp * 64, 64), 64), :]

    def own_rows(j):
        return pltpu.make_async_copy(hidden.at[j], slot(z * 3 + j, 2 * c + y), local_sem.at[j])

    def own_terms(h):
        return pltpu.make_async_copy(
            weights.at[pl.ds(h * CHUNK, CHUNK), :], terms.at[x * 2 + h], local_sem.at[3 + h]
        )

    own_queries = pltpu.make_async_copy(queries, query_rows, local_sem.at[5])

    def side_terms(h):
        return send(weights.at[pl.ds(h * CHUNK, CHUNK), :], terms.at[x * 2 + h], w_s.at[h], w_r.at[h], x_side)

    def side_terms_in(h):
        return send(weights.at[pl.ds(h * CHUNK, CHUNK), :], terms.at[(1 - x) * 2 + h], w_s.at[h], w_r.at[h], x_side)

    def go_up(m, side):
        block, at = slot(m, 2 * c + side), m * 2 + side
        return send(block, block, up_s.at[at], z_r.at[at], above)

    def go_down(m, side):
        block, at = slot(m, 2 * c + side), m * 2 + side
        return send(block, block, down_s.at[at], z_r.at[at], below)

    items = 4 - c

    def item(at):
        extra = at % items == 3
        return jnp.where(extra, 0, (at % items + 1) % 3), jnp.where(extra, 1 - y, y)

    def send_z(at):
        far = at // items
        j, side = item(at)

        @pl.when(jnp.logical_and(z < 3, z - far >= 0))
        def _():
            go_up((z - far) * 3 + j, side).start()

        @pl.when(jnp.logical_and(z > 0, z + far <= 3))
        def _():
            go_down((z + far) * 3 + j, side).start()

    def y_first(j):
        return jnp.logical_and(c == 0, j == 0)

    def go_y(m):
        return send(slot(m, 2 * c + y), slot(m, 2 * c + y), y_s.at[m], y_r.at[m], y_side)

    def come_y(m):
        block = slot(m, 2 * c + 1 - y)
        return send(block, block, y_s.at[m], y_r.at[m], y_side)

    def go_sibling(m, side):
        block = slot(m, 2 * c + side)
        return send(block, block, sib_s.at[m * 2 + side], sib_r.at[m * 2 + side], sibling)

    def come_sibling(m, side):
        block = slot(m, 2 * (1 - c) + side)
        return send(block, block, sib_s.at[m * 2 + side], sib_r.at[m * 2 + side], sibling)

    for j in range(3):
        own_rows(j).start()
    side_terms(0).start()

    def meta_to(i):
        peer = (d + i) % 8
        return send(meta, meta_all.at[d], meta_s.at[i], meta_r.at[d], (v, peer))

    def meta_from(i):
        peer = (d + i) % 8
        return send(meta, meta_all.at[peer], meta_s.at[i], meta_r.at[peer], (v, peer))

    @pl.loop(1, 8)
    def _(i):
        meta_to(i).start()

    meta_all[d] = meta[...]
    for h in range(2):
        own_terms(h).start()
    own_queries.start()
    pooled[...] = jnp.zeros_like(pooled)

    for j in range(3):
        own_rows(j).wait()
    for j in range(2):
        send_z(j)
        go_y(z * 3 + j).start()
    for j in range(3):
        go_sibling(z * 3 + j, y).start()

    for h in range(2):
        own_terms(h).wait()
        turned[x * 2 + h] = terms[x * 2 + h].T

    @pl.loop(1, 8)
    def _(i):
        meta_from(i).wait_recv()

    row_id = lax.broadcasted_iota(jnp.int32, (16, 128), 0)
    mine = d.astype(jnp.float32)
    for side in range(2):
        listed = jnp.zeros((16, 128), jnp.float32)
        for zp in range(4):
            routes = meta_all[2 * zp + side][0:4, :]
            hit = jnp.max(jnp.where(routes == mine, 1.0, 0.0), axis=0, keepdims=True)
            listed = jnp.where(row_id // 4 == zp, hit, listed)
        for t in range(32):
            keep[side * 16:side * 16 + 16, t * 128:(t + 1) * 128] = jnp.broadcast_to(listed[:, t:t + 1], (16, 128))

    def order(n):
        end = jnp.logical_or(z == 0, z == 3)
        step = n - 3
        end_z = jnp.where(z == 0, z + step // 3 + 1, z - step // 3 - 1)
        near = jnp.where(step % 2 == 0, z - 1, z + 1)
        mid_z = jnp.where(n < 9, near, jnp.where(z == 1, 3, 0))
        mid_j = jnp.where(n < 9, step // 2, n - 9)
        zp = jnp.where(n < 3, z, jnp.where(end, end_z, mid_z))
        j = jnp.where(n < 3, n, (jnp.where(end, step % 3, mid_j) + 1) % 3)
        return zp, j

    place = lax.broadcasted_iota(jnp.int32, (8, CHUNK), 0).astype(jnp.float32)

    def pool(n, q):
        zp, j = order(n)
        m = zp * 3 + j
        logits = lax.dot_general(
            rows[m], turned[q], (((1,), (0,)), ((), ())), preferred_element_type=jnp.float32
        )
        for core in range(2):
            length = meta_all[2 * zp + core, pl.ds(4 + j, 1), :]
            length = jnp.concatenate([length] * (CHUNK // 128), axis=1)
            total = jnp.zeros((8, CHUNK), jnp.float32)
            for side in range(2):
                room = length - place - (64 * x + 128 * side).astype(jnp.float32)
                at = 128 * core + 64 * side
                parts = [
                    jnp.where(room > float(8 * i), jnp.maximum(logits[at + 8 * i:at + 8 * i + 8, :], 0.0), 0.0)
                    for i in range(8)
                ]
                while len(parts) > 1:
                    parts = [a + b + a * b for a, b in zip(parts[0::2], parts[1::2])]
                total = total + jnp.log1p(parts[0])
            pooled[q, pl.ds(core * 16 + zp * 4 + j, 1), :] = jnp.sum(total, axis=0, keepdims=True)

    def sums_to(h):
        return send(pooled.at[(1 - x) * 2 + h], sums_in.at[h], sum_s.at[h], sum_r.at[h], x_side)

    def crosses(zp, j):
        return jnp.logical_or(jnp.logical_not(y_first(j)), zp == z)

    @pl.loop(0, 12)
    def _(n):
        zp, jj = order(n)
        m = zp * 3 + jj

        @pl.when(crosses(zp, jj))
        def _():
            come_y(m).wait_recv()
            go_sibling(m, 1 - y).start()

        far = n // items + 1
        j, side = item(n)

        @pl.when(z - far >= 0)
        def _():
            at = (z - far) * 3 + j
            go_up(at, side).wait_recv()
            go_sibling(at, side).start()

        @pl.when(z + far <= 3)
        def _():
            at = (z + far) * 3 + j
            go_down(at, side).wait_recv()
            go_sibling(at, side).start()

        send_z(n + 2)
        ahead = n + 1 + c
        next_z, next_j = order(ahead)

        @pl.when(jnp.logical_and(jnp.logical_and(ahead >= 2, ahead < 12), crosses(next_z, next_j)))
        def _():
            go_y(next_z * 3 + next_j).start()

        come_sibling(m, 0).wait_recv()
        come_sibling(m, 1).wait_recv()

        for h, first in ((0, 4), (1, 9)):
            @pl.when(n == first)
            def _():
                side_terms_in(h).wait_recv()
                if h == 0:
                    side_terms(1).start()
                turned[(1 - x) * 2 + h] = terms[(1 - x) * 2 + h].T

        @pl.loop(0, 4)
        def _(i):
            late = 5 * (n - 9)
            start = jnp.where(i == 1, jnp.where(n < 9, n, late), jnp.where(jnp.logical_and(i == 0, n == 4), 0, n))
            late_stop = jnp.where(n < 9, n, jnp.minimum(late + 5, 12))
            early_stop = jnp.where(jnp.logical_and(i == 0, n < 4), n, n + 1)
            stop = jnp.where(i == 1, late_stop, early_stop)
            q = jnp.where(i < 2, (1 - x) * 2 + i, x * 2 + i - 2)

            def step(at, carry):
                pool(at, q)
                return carry

            lax.fori_loop(start, stop, step, 0)

            @pl.when(jnp.logical_and(n == 11, i < 2))
            def _():
                sums_to(i).start()

    row_32 = lax.broadcasted_iota(jnp.int32, (32, 128), 0)
    length_of = jnp.ones((32, 128), jnp.float32)
    for b in range(8):
        for j in range(3):
            length_of = jnp.where(row_32 == b % 2 * 16 + b // 2 * 4 + j, meta_all[b, 4 + j:5 + j, :], length_of)
    length_wide = jnp.concatenate([length_of] * (CHUNK // 128), axis=1)
    for h in range(2):
        sums_to(h).wait_recv()
        total = pooled[x * 2 + h] + sums_in[h]
        doc_send[:, h * CHUNK:(h + 1) * CHUNK] = (total / length_wide).astype(jnp.bfloat16)

    def doc_to(i):
        return send(doc_send, doc_all.at[d], doc_s.at[i], doc_r.at[d], (v, (d + i) % 8))

    def doc_from(i):
        peer = (d + i) % 8
        return send(doc_send, doc_all.at[peer], doc_s.at[i], doc_r.at[peer], (v, peer))

    @pl.loop(1, 8)
    def _(i):
        doc_to(i).start()

    doc_all[d] = doc_send[...]

    length_sum = jnp.zeros((1, 128), jnp.float32)
    for b in range(8):
        for j in range(3):
            length_sum = length_sum + meta_all[b, 4 + j:5 + j, :]
    average = length_sum / 24.0
    den = saturate * (1.0 - length_slope + length_slope * length_of / average)
    den = jnp.concatenate([den] * 4, axis=1)
    own_queries.wait()

    @pl.loop(1, 8)
    def _(i):
        doc_from(i).wait_recv()

    pick_row = lax.broadcasted_iota(jnp.int32, (8, 32), 0)
    pick_col = lax.broadcasted_iota(jnp.int32, (8, 32), 1)
    pick = jnp.logical_and(pick_col == c * 16 + z * 4 + pick_row, pick_row < 3)
    pick = jnp.where(pick, 1.0, 0.0).astype(jnp.bfloat16)
    for b in range(8):
        cols = slice(b * 512, (b + 1) * 512)
        doc_out[:, cols] = jnp.dot(pick, doc_all[b], preferred_element_type=jnp.float32)
        weight = doc_all[b].astype(jnp.float32)
        scaled = weight * (saturate + 1.0) / (weight + den)
        masked[:, cols] = jnp.where(keep[:, cols] > 0.5, scaled, 0.0).astype(jnp.bfloat16)

    part[...] = lax.dot_general(
        masked[...], query_rows[...], (((1,), (1,)), ((), ())), preferred_element_type=jnp.float32
    )
    for zp in range(4):
        for side in range(2):
            part_send[zp, side * 4:side * 4 + 4, :] = part[side * 16 + zp * 4:side * 16 + zp * 4 + 4, :]

    def part_to(i):
        return send(part_send.at[(v + i) % 4], part_all.at[v], part_s.at[i], part_r.at[v], ((v + i) % 4, d))

    def part_from(i):
        peer = (v + i) % 4
        return send(part_send.at[peer], part_all.at[peer], part_s.at[i], part_r.at[peer], (peer, d))

    for i in range(1, 4):
        part_to(i).start()
    part_all[v] = part_send[v]

    for h in range(2):
        side_terms(h).wait_send()
        sums_to(h).wait_send()

    @pl.loop(0, 12)
    def _(m):
        zp, j = m // 3, m % 3
        crossed = jnp.logical_and(y_first(j), zp != z)
        for side, there in ((y, True), (1 - y, y_first(j))):
            @pl.when(jnp.logical_and(there, jnp.logical_and(z < 3, zp <= z)))
            def _():
                go_up(m, side).wait_send()

            @pl.when(jnp.logical_and(there, jnp.logical_and(z > 0, zp >= z)))
            def _():
                go_down(m, side).wait_send()

        @pl.when(jnp.logical_not(crossed))
        def _():
            go_y(m).wait_send()

        go_sibling(m, 0).wait_send()
        go_sibling(m, 1).wait_send()

    @pl.loop(1, 8)
    def _(i):
        meta_to(i).wait_send()

    @pl.loop(1, 8)
    def _(i):
        doc_to(i).wait_send()

    for i in range(1, 4):
        part_from(i).wait_recv()
        part_to(i).wait_send()
    score_out[...] = (part_all[0] + part_all[1]) + (part_all[2] + part_all[3])


def local_kernel(hidden, w_vocab, lengths, query_terms, tile_routes):
    routes = jnp.pad(tile_routes[0].T.astype(jnp.float32), ((0, 0), (0, 96)))
    lens = jnp.broadcast_to(lengths.astype(jnp.float32)[:, None], (3, 128))
    meta = jnp.concatenate([routes, lens, jnp.zeros((1, 128), jnp.float32)], axis=0)
    width = hidden.shape[2]
    any_space, vmem = pl.BlockSpec(memory_space=pl.ANY), pl.BlockSpec(memory_space=pltpu.VMEM)
    dma = lambda count: pltpu.SemaphoreType.DMA((count,))
    docs, scores = pl.pallas_call(
        head_kernel,
        out_shape=(
            jax.ShapeDtypeStruct((8, 4096), jnp.float32),
            jax.ShapeDtypeStruct((8, 128), jnp.float32),
        ),
        in_specs=[any_space, any_space, any_space, vmem],
        out_specs=(vmem, vmem),
        scratch_shapes=[
            pltpu.VMEM((12, 256, width), jnp.bfloat16),
            pltpu.VMEM((4, CHUNK, width), jnp.bfloat16),
            pltpu.VMEM((4, width, CHUNK), jnp.bfloat16),
            pltpu.VMEM((128, 4096), jnp.bfloat16),
            pltpu.VMEM((8, 8, 128), jnp.float32),
            pltpu.VMEM((32, 4096), jnp.float32),
            pltpu.VMEM((4, 32, CHUNK), jnp.float32),
            pltpu.VMEM((32, 512), jnp.bfloat16),
            pltpu.VMEM((8, 32, 512), jnp.bfloat16),
            pltpu.VMEM((32, 4096), jnp.bfloat16),
            pltpu.VMEM((32, 128), jnp.float32),
            pltpu.VMEM((4, 8, 128), jnp.float32),
            pltpu.VMEM((4, 8, 128), jnp.float32),
            pltpu.VMEM((2, 32, CHUNK), jnp.float32),
            dma(6), dma(2), dma(2), dma(24), dma(24), dma(24), dma(12), dma(12), dma(24), dma(24),
            dma(8), dma(8), dma(8), dma(8), dma(4), dma(4), dma(2), dma(2),
        ],
        compiler_params=pltpu.CompilerParams(
            collective_id=0, has_side_effects=True, vmem_limit_bytes=60 * 1024 * 1024
        ),
    )(hidden, w_vocab, query_terms, meta)
    doc_terms = docs[:3].astype(jnp.bfloat16)
    return doc_terms, scores.reshape(2, 4, 128)[:, :3].reshape(6, 128).T


def solution(mesh):
    shape = dict(mesh.shape)
    body = local_kernel if (shape["vocab"], shape["docs"]) == (4, 8) else local
    return jax.shard_map(
        body,
        mesh=mesh,
        in_specs=(
            P("docs", "vocab", None),
            P(("vocab", "docs"), None),
            P("docs"),
            P("docs", "vocab"),
            P("docs", "vocab", None),
        ),
        out_specs=(P("docs", "vocab"), P("docs", "vocab")),
        check_vma=False,
    )
```

```python
import jax
import jax.numpy as jnp
from jax import lax
from jax.experimental import pallas as pl
from jax.experimental.pallas import tpu as pltpu
from jax.sharding import PartitionSpec as P

saturate = 1.2
length_slope = 0.75


def pooled_rows(passage_rows, weights, lens_here):
    logits = lax.dot_general(
        passage_rows, weights, (((2,), (1,)), ((), ())), preferred_element_type=jnp.float32
    )
    places = lax.broadcasted_iota(jnp.int32, logits.shape, 1)
    activity = jnp.where(
        places < lens_here[:, None, None], jnp.log1p(jnp.maximum(logits, 0.0)), 0.0
    )
    return jnp.sum(activity, axis=1) / lens_here.astype(jnp.float32)[:, None]


def local(hidden, w_vocab, lengths, query_terms, tile_routes):
    members = lax.axis_size("docs")
    local_count = hidden.shape[0]
    lens_all = lax.all_gather(lengths, "docs", axis=0, tiled=True)
    passage_total = lens_all.shape[0]
    average = jnp.sum(lens_all.astype(jnp.float32)) / passage_total
    full_rows = lax.all_gather(hidden, "vocab", axis=1, tiled=True)
    doc_terms = pooled_rows(
        full_rows, lax.all_gather(w_vocab, "docs", axis=0, tiled=True), lengths
    ).astype(jnp.bfloat16)
    weight = doc_terms.astype(jnp.float32)
    denominator = saturate * (
        1.0 - length_slope + length_slope * lengths.astype(jnp.float32) / average
    )
    scaled = (weight * (saturate + 1.0) / (weight + denominator[:, None])).astype(jnp.bfloat16)
    term_count = scaled.shape[1]
    tile_count = term_count // 128
    my_routes = tile_routes[0]
    fanout = my_routes.shape[1]
    capacity = min(tile_count, max(4, 2 * tile_count * fanout // members))
    owners = lax.broadcasted_iota(jnp.int32, (1, 1, members), 2)
    is_listed = jnp.any(my_routes[:, :, None] == owners, axis=1)
    slot_index = jnp.cumsum(is_listed.astype(jnp.int32), axis=0) - 1
    slot_ids = lax.broadcasted_iota(jnp.int32, (1, capacity, 1), 1)
    selector = (is_listed.T[:, None, :] & (slot_index.T[:, None, :] == slot_ids)).astype(
        jnp.bfloat16
    )
    blocks = scaled.reshape(local_count, tile_count, 128)
    outgoing = jnp.einsum(
        "oct,ptk->ocpk", selector, blocks, preferred_element_type=jnp.float32
    ).astype(jnp.bfloat16)
    tile_ids = lax.broadcasted_iota(jnp.float32, (1, 1, tile_count), 2)
    labels = jnp.sum(selector.astype(jnp.float32) * tile_ids, axis=2).astype(jnp.bfloat16)
    arrived, labels_in = (
        lax.all_to_all(outgoing, "docs", split_axis=0, concat_axis=0, tiled=True),
        lax.all_to_all(labels, "docs", split_axis=0, concat_axis=0, tiled=True),
    )
    placing = (labels_in.astype(jnp.float32)[:, :, None] == tile_ids).astype(jnp.bfloat16)
    masked = jnp.einsum(
        "bct,bcpk->bptk", placing, arrived, preferred_element_type=jnp.float32
    ).astype(jnp.bfloat16)
    masked = masked.reshape(passage_total, term_count)
    partial_value = lax.dot_general(
        query_terms, masked, (((1,), (1,)), ((), ())), preferred_element_type=jnp.float32
    )
    scores = lax.psum_scatter(partial_value, "vocab", scatter_dimension=1, tiled=True)
    return (doc_terms, scores)


CHUNK = 256
MESH = pl.DeviceIdType.MESH


def head_kernel(
    hidden, weights, queries, meta, doc_out, score_out,
    rows, terms, turned, query_rows, meta_all, keep, pooled, doc_send, doc_all, masked, part, part_send, part_all, sums_in,
    local_sem, w_s, w_r, up_s, down_s, z_r, y_s, y_r, sib_s, sib_r,
    meta_s, meta_r, doc_s, doc_r, part_s, part_r, sum_s, sum_r,
):
    v, d = lax.axis_index("vocab"), lax.axis_index("docs")
    x, y, z, c = v % 2, v // 2, d // 2, d % 2
    x_side, y_side = (2 * y + 1 - x, d), (2 * (1 - y) + x, d)
    sibling = (v, 2 * z + 1 - c)
    above, below = (v, d + 2), (v, d - 2)

    def send(src, dst, s_sem, r_sem, to):
        return pltpu.make_async_remote_copy(
            src_ref=src, dst_ref=dst, send_sem=s_sem, recv_sem=r_sem, device_id=to, device_id_type=MESH
        )

    barrier = pltpu.get_barrier_semaphore()

    @pl.loop(1, 8)
    def _(i):
        pl.semaphore_signal(barrier, inc=1, device_id=(v, (d + i) % 8), device_id_type=MESH)

    for i in range(1, 4):
        pl.semaphore_signal(barrier, inc=1, device_id=((v + i) % 4, d), device_id_type=MESH)
    pl.semaphore_wait(barrier, 10)

    def slot(m, vp):
        return rows.at[m, pl.ds(pl.multiple_of(vp * 64, 64), 64), :]

    def own_rows(j):
        return pltpu.make_async_copy(hidden.at[j], slot(z * 3 + j, 2 * c + y), local_sem.at[j])

    def own_terms(h):
        return pltpu.make_async_copy(
            weights.at[pl.ds(h * CHUNK, CHUNK), :], terms.at[x * 2 + h], local_sem.at[3 + h]
        )

    own_queries = pltpu.make_async_copy(queries, query_rows, local_sem.at[5])

    def side_terms(h):
        return send(weights.at[pl.ds(h * CHUNK, CHUNK), :], terms.at[x * 2 + h], w_s.at[h], w_r.at[h], x_side)

    def side_terms_in(h):
        return send(weights.at[pl.ds(h * CHUNK, CHUNK), :], terms.at[(1 - x) * 2 + h], w_s.at[h], w_r.at[h], x_side)

    def go_up(m, side):
        block, at = slot(m, 2 * c + side), m * 2 + side
        return send(block, block, up_s.at[at], z_r.at[at], above)

    def go_down(m, side):
        block, at = slot(m, 2 * c + side), m * 2 + side
        return send(block, block, down_s.at[at], z_r.at[at], below)

    items = 4 - c

    def item(at):
        extra = at % items == 3
        return jnp.where(extra, 0, (at % items + 1) % 3), jnp.where(extra, 1 - y, y)

    def send_z(at):
        far = at // items
        j, side = item(at)

        @pl.when(jnp.logical_and(z < 3, z - far >= 0))
        def _():
            go_up((z - far) * 3 + j, side).start()

        @pl.when(jnp.logical_and(z > 0, z + far <= 3))
        def _():
            go_down((z + far) * 3 + j, side).start()

    def y_first(j):
        return jnp.logical_and(c == 0, j == 0)

    def go_y(m):
        return send(slot(m, 2 * c + y), slot(m, 2 * c + y), y_s.at[m], y_r.at[m], y_side)

    def come_y(m):
        block = slot(m, 2 * c + 1 - y)
        return send(block, block, y_s.at[m], y_r.at[m], y_side)

    def go_sibling(m, side):
        block = slot(m, 2 * c + side)
        return send(block, block, sib_s.at[m * 2 + side], sib_r.at[m * 2 + side], sibling)

    def come_sibling(m, side):
        block = slot(m, 2 * (1 - c) + side)
        return send(block, block, sib_s.at[m * 2 + side], sib_r.at[m * 2 + side], sibling)

    for j in range(3):
        own_rows(j).start()
    side_terms(0).start()

    def meta_to(i):
        peer = (d + i) % 8
        return send(meta, meta_all.at[d], meta_s.at[i], meta_r.at[d], (v, peer))

    def meta_from(i):
        peer = (d + i) % 8
        return send(meta, meta_all.at[peer], meta_s.at[i], meta_r.at[peer], (v, peer))

    @pl.loop(1, 8)
    def _(i):
        meta_to(i).start()

    meta_all[d] = meta[...]
    for h in range(2):
        own_terms(h).start()
    own_queries.start()
    pooled[...] = jnp.zeros_like(pooled)

    for j in range(3):
        own_rows(j).wait()
    for j in range(2):
        send_z(j)
        go_y(z * 3 + j).start()
    for j in range(3):
        go_sibling(z * 3 + j, y).start()

    for h in range(2):
        own_terms(h).wait()
        turned[x * 2 + h] = terms[x * 2 + h].T

    @pl.loop(1, 8)
    def _(i):
        meta_from(i).wait_recv()

    row_id = lax.broadcasted_iota(jnp.int32, (16, 128), 0)
    mine = d.astype(jnp.float32)
    for side in range(2):
        listed = jnp.zeros((16, 128), jnp.float32)
        for zp in range(4):
            routes = meta_all[2 * zp + side][0:4, :]
            hit = jnp.max(jnp.where(routes == mine, 1.0, 0.0), axis=0, keepdims=True)
            listed = jnp.where(row_id // 4 == zp, hit, listed)
        for t in range(32):
            keep[side * 16:side * 16 + 16, t * 128:(t + 1) * 128] = jnp.broadcast_to(listed[:, t:t + 1], (16, 128))

    def order(n):
        end = jnp.logical_or(z == 0, z == 3)
        step = n - 3
        end_z = jnp.where(z == 0, z + step // 3 + 1, z - step // 3 - 1)
        near = jnp.where(step % 2 == 0, z - 1, z + 1)
        mid_z = jnp.where(n < 9, near, jnp.where(z == 1, 3, 0))
        mid_j = jnp.where(n < 9, step // 2, n - 9)
        zp = jnp.where(n < 3, z, jnp.where(end, end_z, mid_z))
        j = jnp.where(n < 3, n, (jnp.where(end, step % 3, mid_j) + 1) % 3)
        return zp, j

    place = lax.broadcasted_iota(jnp.int32, (8, CHUNK), 0).astype(jnp.float32)

    def pool(n, q):
        zp, j = order(n)
        m = zp * 3 + j
        logits = lax.dot_general(
            rows[m], turned[q], (((1,), (0,)), ((), ())), preferred_element_type=jnp.float32
        )
        for core in range(2):
            length = meta_all[2 * zp + core, pl.ds(4 + j, 1), :]
            length = jnp.concatenate([length] * (CHUNK // 128), axis=1)
            total = jnp.zeros((8, CHUNK), jnp.float32)
            for side in range(2):
                room = length - place - (64 * x + 128 * side).astype(jnp.float32)
                at = 128 * core + 64 * side
                parts = [
                    jnp.where(room > float(8 * i), jnp.maximum(logits[at + 8 * i:at + 8 * i + 8, :], 0.0), 0.0)
                    for i in range(8)
                ]
                while len(parts) > 1:
                    parts = [a + b + a * b for a, b in zip(parts[0::2], parts[1::2])]
                total = total + jnp.log1p(parts[0])
            pooled[q, pl.ds(core * 16 + zp * 4 + j, 1), :] = jnp.sum(total, axis=0, keepdims=True)

    def sums_to(h):
        return send(pooled.at[(1 - x) * 2 + h], sums_in.at[h], sum_s.at[h], sum_r.at[h], x_side)

    def crosses(zp, j):
        return jnp.logical_or(jnp.logical_not(y_first(j)), zp == z)

    @pl.loop(0, 12)
    def _(n):
        zp, jj = order(n)
        m = zp * 3 + jj

        @pl.when(crosses(zp, jj))
        def _():
            come_y(m).wait_recv()
            go_sibling(m, 1 - y).start()

        far = n // items + 1
        j, side = item(n)

        @pl.when(z - far >= 0)
        def _():
            at = (z - far) * 3 + j
            go_up(at, side).wait_recv()
            go_sibling(at, side).start()

        @pl.when(z + far <= 3)
        def _():
            at = (z + far) * 3 + j
            go_down(at, side).wait_recv()
            go_sibling(at, side).start()

        send_z(n + 2)
        ahead = jnp.where(jnp.logical_and(c == 0, n > 7), n + 1, n + 2)
        skip = jnp.logical_and(c == 0, n == 7)
        next_z, next_j = order(ahead)
        crossing = jnp.logical_and(ahead < 12, crosses(next_z, next_j))

        @pl.when(jnp.logical_and(crossing, jnp.logical_not(skip)))
        def _():
            go_y(next_z * 3 + next_j).start()

        come_sibling(m, 0).wait_recv()
        come_sibling(m, 1).wait_recv()

        for h, first in ((0, 4), (1, 9)):
            @pl.when(n == first)
            def _():
                side_terms_in(h).wait_recv()
                if h == 0:
                    side_terms(1).start()
                turned[(1 - x) * 2 + h] = terms[(1 - x) * 2 + h].T

        @pl.loop(0, 4)
        def _(i):
            late = 5 * (n - 9)
            start = jnp.where(i == 1, jnp.where(n < 9, n, late), jnp.where(jnp.logical_and(i == 0, n == 4), 0, n))
            late_stop = jnp.where(n < 9, n, jnp.minimum(late + 5, 12))
            early_stop = jnp.where(jnp.logical_and(i == 0, n < 4), n, n + 1)
            stop = jnp.where(i == 1, late_stop, early_stop)
            q = jnp.where(i < 2, (1 - x) * 2 + i, x * 2 + i - 2)

            def step(at, carry):
                pool(at, q)
                return carry

            lax.fori_loop(start, stop, step, 0)

            @pl.when(jnp.logical_and(n == 11, i < 2))
            def _():
                sums_to(i).start()

    row_32 = lax.broadcasted_iota(jnp.int32, (32, 128), 0)
    length_of = jnp.ones((32, 128), jnp.float32)
    for b in range(8):
        for j in range(3):
            length_of = jnp.where(row_32 == b % 2 * 16 + b // 2 * 4 + j, meta_all[b, 4 + j:5 + j, :], length_of)
    length_wide = jnp.concatenate([length_of] * (CHUNK // 128), axis=1)
    for h in range(2):
        sums_to(h).wait_recv()
        total = pooled[x * 2 + h] + sums_in[h]
        doc_send[:, h * CHUNK:(h + 1) * CHUNK] = (total / length_wide).astype(jnp.bfloat16)

    def doc_to(i):
        return send(doc_send, doc_all.at[d], doc_s.at[i], doc_r.at[d], (v, (d + i) % 8))

    def doc_from(i):
        peer = (d + i) % 8
        return send(doc_send, doc_all.at[peer], doc_s.at[i], doc_r.at[peer], (v, peer))

    @pl.loop(1, 8)
    def _(i):
        doc_to(i).start()

    doc_all[d] = doc_send[...]

    length_sum = jnp.zeros((1, 128), jnp.float32)
    for b in range(8):
        for j in range(3):
            length_sum = length_sum + meta_all[b, 4 + j:5 + j, :]
    average = length_sum / 24.0
    den = saturate * (1.0 - length_slope + length_slope * length_of / average)
    den = jnp.concatenate([den] * 4, axis=1)
    own_queries.wait()

    @pl.loop(1, 8)
    def _(i):
        doc_from(i).wait_recv()

    pick_row = lax.broadcasted_iota(jnp.int32, (8, 32), 0)
    pick_col = lax.broadcasted_iota(jnp.int32, (8, 32), 1)
    pick = jnp.logical_and(pick_col == c * 16 + z * 4 + pick_row, pick_row < 3)
    pick = jnp.where(pick, 1.0, 0.0).astype(jnp.bfloat16)
    for b in range(8):
        cols = slice(b * 512, (b + 1) * 512)
        doc_out[:, cols] = jnp.dot(pick, doc_all[b], preferred_element_type=jnp.float32)
        weight = doc_all[b].astype(jnp.float32)
        scaled = weight * (saturate + 1.0) / (weight + den)
        masked[:, cols] = jnp.where(keep[:, cols] > 0.5, scaled, 0.0).astype(jnp.bfloat16)

    part[...] = lax.dot_general(
        masked[...], query_rows[...], (((1,), (1,)), ((), ())), preferred_element_type=jnp.float32
    )
    for zp in range(4):
        for side in range(2):
            part_send[zp, side * 4:side * 4 + 4, :] = part[side * 16 + zp * 4:side * 16 + zp * 4 + 4, :]

    def part_to(i):
        return send(part_send.at[(v + i) % 4], part_all.at[v], part_s.at[i], part_r.at[v], ((v + i) % 4, d))

    def part_from(i):
        peer = (v + i) % 4
        return send(part_send.at[peer], part_all.at[peer], part_s.at[i], part_r.at[peer], (peer, d))

    for i in range(1, 4):
        part_to(i).start()
    part_all[v] = part_send[v]

    for h in range(2):
        side_terms(h).wait_send()
        sums_to(h).wait_send()

    @pl.loop(0, 12)
    def _(m):
        zp, j = m // 3, m % 3
        crossed = jnp.logical_and(y_first(j), zp != z)
        for side, there in ((y, True), (1 - y, y_first(j))):
            @pl.when(jnp.logical_and(there, jnp.logical_and(z < 3, zp <= z)))
            def _():
                go_up(m, side).wait_send()

            @pl.when(jnp.logical_and(there, jnp.logical_and(z > 0, zp >= z)))
            def _():
                go_down(m, side).wait_send()

        @pl.when(jnp.logical_not(crossed))
        def _():
            go_y(m).wait_send()

        go_sibling(m, 0).wait_send()
        go_sibling(m, 1).wait_send()

    @pl.loop(1, 8)
    def _(i):
        meta_to(i).wait_send()

    @pl.loop(1, 8)
    def _(i):
        doc_to(i).wait_send()

    for i in range(1, 4):
        part_from(i).wait_recv()
        part_to(i).wait_send()
    score_out[...] = (part_all[0] + part_all[1]) + (part_all[2] + part_all[3])


def local_kernel(hidden, w_vocab, lengths, query_terms, tile_routes):
    routes = jnp.pad(tile_routes[0].T.astype(jnp.float32), ((0, 0), (0, 96)))
    lens = jnp.broadcast_to(lengths.astype(jnp.float32)[:, None], (3, 128))
    meta = jnp.concatenate([routes, lens, jnp.zeros((1, 128), jnp.float32)], axis=0)
    width = hidden.shape[2]
    any_space, vmem = pl.BlockSpec(memory_space=pl.ANY), pl.BlockSpec(memory_space=pltpu.VMEM)
    dma = lambda count: pltpu.SemaphoreType.DMA((count,))
    docs, scores = pl.pallas_call(
        head_kernel,
        out_shape=(
            jax.ShapeDtypeStruct((8, 4096), jnp.float32),
            jax.ShapeDtypeStruct((8, 128), jnp.float32),
        ),
        in_specs=[any_space, any_space, any_space, vmem],
        out_specs=(vmem, vmem),
        scratch_shapes=[
            pltpu.VMEM((12, 256, width), jnp.bfloat16),
            pltpu.VMEM((4, CHUNK, width), jnp.bfloat16),
            pltpu.VMEM((4, width, CHUNK), jnp.bfloat16),
            pltpu.VMEM((128, 4096), jnp.bfloat16),
            pltpu.VMEM((8, 8, 128), jnp.float32),
            pltpu.VMEM((32, 4096), jnp.float32),
            pltpu.VMEM((4, 32, CHUNK), jnp.float32),
            pltpu.VMEM((32, 512), jnp.bfloat16),
            pltpu.VMEM((8, 32, 512), jnp.bfloat16),
            pltpu.VMEM((32, 4096), jnp.bfloat16),
            pltpu.VMEM((32, 128), jnp.float32),
            pltpu.VMEM((4, 8, 128), jnp.float32),
            pltpu.VMEM((4, 8, 128), jnp.float32),
            pltpu.VMEM((2, 32, CHUNK), jnp.float32),
            dma(6), dma(2), dma(2), dma(24), dma(24), dma(24), dma(12), dma(12), dma(24), dma(24),
            dma(8), dma(8), dma(8), dma(8), dma(4), dma(4), dma(2), dma(2),
        ],
        compiler_params=pltpu.CompilerParams(
            collective_id=0, has_side_effects=True, vmem_limit_bytes=60 * 1024 * 1024
        ),
    )(hidden, w_vocab, query_terms, meta)
    doc_terms = docs[:3].astype(jnp.bfloat16)
    return doc_terms, scores.reshape(2, 4, 128)[:, :3].reshape(6, 128).T


def solution(mesh):
    shape = dict(mesh.shape)
    body = local_kernel if (shape["vocab"], shape["docs"]) == (4, 8) else local
    return jax.shard_map(
        body,
        mesh=mesh,
        in_specs=(
            P("docs", "vocab", None),
            P(("vocab", "docs"), None),
            P("docs"),
            P("docs", "vocab"),
            P("docs", "vocab", None),
        ),
        out_specs=(P("docs", "vocab"), P("docs", "vocab")),
        check_vma=False,
    )
```

```python
import jax
import jax.numpy as jnp
from jax import lax
from jax.experimental import pallas as pl
from jax.experimental.pallas import tpu as pltpu
from jax.sharding import PartitionSpec as P

saturate = 1.2
length_slope = 0.75


def pooled_rows(passage_rows, weights, lens_here):
    logits = lax.dot_general(
        passage_rows, weights, (((2,), (1,)), ((), ())), preferred_element_type=jnp.float32
    )
    places = lax.broadcasted_iota(jnp.int32, logits.shape, 1)
    activity = jnp.where(
        places < lens_here[:, None, None], jnp.log1p(jnp.maximum(logits, 0.0)), 0.0
    )
    return jnp.sum(activity, axis=1) / lens_here.astype(jnp.float32)[:, None]


def local(hidden, w_vocab, lengths, query_terms, tile_routes):
    members = lax.axis_size("docs")
    local_count = hidden.shape[0]
    lens_all = lax.all_gather(lengths, "docs", axis=0, tiled=True)
    passage_total = lens_all.shape[0]
    average = jnp.sum(lens_all.astype(jnp.float32)) / passage_total
    full_rows = lax.all_gather(hidden, "vocab", axis=1, tiled=True)
    doc_terms = pooled_rows(
        full_rows, lax.all_gather(w_vocab, "docs", axis=0, tiled=True), lengths
    ).astype(jnp.bfloat16)
    weight = doc_terms.astype(jnp.float32)
    denominator = saturate * (
        1.0 - length_slope + length_slope * lengths.astype(jnp.float32) / average
    )
    scaled = (weight * (saturate + 1.0) / (weight + denominator[:, None])).astype(jnp.bfloat16)
    term_count = scaled.shape[1]
    tile_count = term_count // 128
    my_routes = tile_routes[0]
    fanout = my_routes.shape[1]
    capacity = min(tile_count, max(4, 2 * tile_count * fanout // members))
    owners = lax.broadcasted_iota(jnp.int32, (1, 1, members), 2)
    is_listed = jnp.any(my_routes[:, :, None] == owners, axis=1)
    slot_index = jnp.cumsum(is_listed.astype(jnp.int32), axis=0) - 1
    slot_ids = lax.broadcasted_iota(jnp.int32, (1, capacity, 1), 1)
    selector = (is_listed.T[:, None, :] & (slot_index.T[:, None, :] == slot_ids)).astype(
        jnp.bfloat16
    )
    blocks = scaled.reshape(local_count, tile_count, 128)
    outgoing = jnp.einsum(
        "oct,ptk->ocpk", selector, blocks, preferred_element_type=jnp.float32
    ).astype(jnp.bfloat16)
    tile_ids = lax.broadcasted_iota(jnp.float32, (1, 1, tile_count), 2)
    labels = jnp.sum(selector.astype(jnp.float32) * tile_ids, axis=2).astype(jnp.bfloat16)
    arrived, labels_in = (
        lax.all_to_all(outgoing, "docs", split_axis=0, concat_axis=0, tiled=True),
        lax.all_to_all(labels, "docs", split_axis=0, concat_axis=0, tiled=True),
    )
    placing = (labels_in.astype(jnp.float32)[:, :, None] == tile_ids).astype(jnp.bfloat16)
    masked = jnp.einsum(
        "bct,bcpk->bptk", placing, arrived, preferred_element_type=jnp.float32
    ).astype(jnp.bfloat16)
    masked = masked.reshape(passage_total, term_count)
    partial_value = lax.dot_general(
        query_terms, masked, (((1,), (1,)), ((), ())), preferred_element_type=jnp.float32
    )
    scores = lax.psum_scatter(partial_value, "vocab", scatter_dimension=1, tiled=True)
    return (doc_terms, scores)


CHUNK = 256
MESH = pl.DeviceIdType.MESH


def head_kernel(
    hidden, weights, queries, meta, doc_out, score_out,
    rows, terms, turned, query_rows, meta_all, keep, pooled, doc_send, doc_all, masked, part, part_send, part_all, sums_in,
    local_sem, w_s, w_r, up_s, down_s, z_r, y_s, y_r, sib_s, sib_r,
    meta_s, meta_r, doc_s, doc_r, part_s, part_r, sum_s, sum_r,
):
    v, d = lax.axis_index("vocab"), lax.axis_index("docs")
    x, y, z, c = v % 2, v // 2, d // 2, d % 2
    x_side, y_side = (2 * y + 1 - x, d), (2 * (1 - y) + x, d)
    sibling = (v, 2 * z + 1 - c)
    above, below = (v, d + 2), (v, d - 2)

    def send(src, dst, s_sem, r_sem, to):
        return pltpu.make_async_remote_copy(
            src_ref=src, dst_ref=dst, send_sem=s_sem, recv_sem=r_sem, device_id=to, device_id_type=MESH
        )

    barrier = pltpu.get_barrier_semaphore()

    @pl.loop(1, 8)
    def _(i):
        pl.semaphore_signal(barrier, inc=1, device_id=(v, (d + i) % 8), device_id_type=MESH)

    for i in range(1, 4):
        pl.semaphore_signal(barrier, inc=1, device_id=((v + i) % 4, d), device_id_type=MESH)
    pl.semaphore_wait(barrier, 10)

    def slot(m, vp):
        return rows.at[m, pl.ds(pl.multiple_of(vp * 64, 64), 64), :]

    def own_rows(j):
        return pltpu.make_async_copy(hidden.at[j], slot(z * 3 + j, 2 * c + y), local_sem.at[j])

    own_terms = pltpu.make_async_copy(weights, terms.at[x], local_sem.at[3])
    own_queries = pltpu.make_async_copy(queries, query_rows, local_sem.at[4])

    side_terms = send(weights, terms.at[x], w_s.at[0], w_r.at[0], x_side)
    side_terms_in = send(weights, terms.at[1 - x], w_s.at[0], w_r.at[0], x_side)

    def go_up(m, side):
        block, at = slot(m, 2 * c + side), m * 2 + side
        return send(block, block, up_s.at[at], z_r.at[at], above)

    def go_down(m, side):
        block, at = slot(m, 2 * c + side), m * 2 + side
        return send(block, block, down_s.at[at], z_r.at[at], below)

    items = 4 - c

    def item(at):
        extra = at % items == 3
        return jnp.where(extra, 0, (at % items + 1) % 3), jnp.where(extra, 1 - y, y)

    def send_z(at):
        far = at // items
        j, side = item(at)

        @pl.when(jnp.logical_and(z < 3, z - far >= 0))
        def _():
            go_up((z - far) * 3 + j, side).start()

        @pl.when(jnp.logical_and(z > 0, z + far <= 3))
        def _():
            go_down((z + far) * 3 + j, side).start()

    def y_first(j):
        return jnp.logical_and(c == 0, j == 0)

    def go_y(m):
        return send(slot(m, 2 * c + y), slot(m, 2 * c + y), y_s.at[m], y_r.at[m], y_side)

    def come_y(m):
        block = slot(m, 2 * c + 1 - y)
        return send(block, block, y_s.at[m], y_r.at[m], y_side)

    def go_sibling(m, side):
        block = slot(m, 2 * c + side)
        return send(block, block, sib_s.at[m * 2 + side], sib_r.at[m * 2 + side], sibling)

    def come_sibling(m, side):
        block = slot(m, 2 * (1 - c) + side)
        return send(block, block, sib_s.at[m * 2 + side], sib_r.at[m * 2 + side], sibling)

    for j in range(3):
        own_rows(j).start()
    side_terms.start()

    def meta_to(i):
        peer = (d + i) % 8
        return send(meta, meta_all.at[d], meta_s.at[i], meta_r.at[d], (v, peer))

    def meta_from(i):
        peer = (d + i) % 8
        return send(meta, meta_all.at[peer], meta_s.at[i], meta_r.at[peer], (v, peer))

    @pl.loop(1, 8)
    def _(i):
        meta_to(i).start()

    meta_all[d] = meta[...]
    own_terms.start()
    own_queries.start()
    pooled[...] = jnp.zeros_like(pooled)

    for j in range(3):
        own_rows(j).wait()
    for j in range(2):
        send_z(j)
        go_y(z * 3 + j).start()
    for j in range(3):
        go_sibling(z * 3 + j, y).start()

    own_terms.wait()
    turned[x] = terms[x].T

    @pl.loop(1, 8)
    def _(i):
        meta_from(i).wait_recv()

    row_id = lax.broadcasted_iota(jnp.int32, (16, 128), 0)
    mine = d.astype(jnp.float32)
    for side in range(2):
        listed = jnp.zeros((16, 128), jnp.float32)
        for zp in range(4):
            routes = meta_all[2 * zp + side][0:4, :]
            hit = jnp.max(jnp.where(routes == mine, 1.0, 0.0), axis=0, keepdims=True)
            listed = jnp.where(row_id // 4 == zp, hit, listed)
        for t in range(32):
            keep[side * 16:side * 16 + 16, t * 128:(t + 1) * 128] = jnp.broadcast_to(listed[:, t:t + 1], (16, 128))

    def order(n):
        end = jnp.logical_or(z == 0, z == 3)
        step = n - 3
        end_z = jnp.where(z == 0, z + step // 3 + 1, z - step // 3 - 1)
        near = jnp.where(step % 2 == 0, z - 1, z + 1)
        mid_z = jnp.where(n < 9, near, jnp.where(z == 1, 3, 0))
        mid_j = jnp.where(n < 9, step // 2, n - 9)
        zp = jnp.where(n < 3, z, jnp.where(end, end_z, mid_z))
        j = jnp.where(n < 3, n, (jnp.where(end, step % 3, mid_j) + 1) % 3)
        return zp, j

    place = lax.broadcasted_iota(jnp.int32, (8, CHUNK), 0).astype(jnp.float32)

    def pool(n, group):
        zp, j = order(n)
        m = zp * 3 + j
        for half in range(0, 512, CHUNK):
            logits = jnp.dot(rows[m], turned[group, :, half:half + CHUNK], preferred_element_type=jnp.float32)
            for core in range(2):
                length = meta_all[2 * zp + core, pl.ds(4 + j, 1), :]
                length = jnp.concatenate([length] * (CHUNK // 128), axis=1)
                total = jnp.zeros((8, CHUNK), jnp.float32)
                for side in range(2):
                    room = length - place - (64 * x + 128 * side).astype(jnp.float32)
                    at = 128 * core + 64 * side
                    parts = [
                        jnp.where(room > float(8 * i), jnp.maximum(logits[at + 8 * i:at + 8 * i + 8, :], 0.0), 0.0)
                        for i in range(8)
                    ]
                    while len(parts) > 1:
                        parts = [a + b + a * b for a, b in zip(parts[0::2], parts[1::2])]
                    total = total + jnp.log1p(parts[0])
                row = pl.ds(core * 16 + zp * 4 + j, 1)
                pooled[group, row, half:half + CHUNK] = jnp.sum(total, axis=0, keepdims=True)

    sums_to = send(pooled.at[1 - x], sums_in, sum_s.at[0], sum_r.at[0], x_side)

    def crosses(zp, j):
        return jnp.logical_or(jnp.logical_not(y_first(j)), zp == z)

    @pl.loop(0, 12)
    def _(n):
        zp, jj = order(n)
        m = zp * 3 + jj

        @pl.when(crosses(zp, jj))
        def _():
            come_y(m).wait_recv()
            go_sibling(m, 1 - y).start()

        far = n // items + 1
        j, side = item(n)

        @pl.when(z - far >= 0)
        def _():
            at = (z - far) * 3 + j
            go_up(at, side).wait_recv()
            go_sibling(at, side).start()

        @pl.when(z + far <= 3)
        def _():
            at = (z + far) * 3 + j
            go_down(at, side).wait_recv()
            go_sibling(at, side).start()

        send_z(n + 2)
        ahead = jnp.where(jnp.logical_and(c == 0, n > 7), n + 1, n + 2)
        skip = jnp.logical_and(c == 0, n == 7)
        next_z, next_j = order(ahead)
        crossing = jnp.logical_and(ahead < 12, crosses(next_z, next_j))

        @pl.when(jnp.logical_and(crossing, jnp.logical_not(skip)))
        def _():
            go_y(next_z * 3 + next_j).start()

        come_sibling(m, 0).wait_recv()
        come_sibling(m, 1).wait_recv()

        @pl.when(n == 7)
        def _():
            side_terms_in.wait_recv()
            turned[1 - x] = terms[1 - x].T

        @pl.loop(0, 2)
        def _(i):
            late = 3 * (n - 7) - n // 11
            late_stop = jnp.minimum(3 * (n - 6) - (n + 1) // 11, 12)
            start = jnp.where(i == 1, n, jnp.where(n < 7, 0, late))
            stop = jnp.where(i == 1, n + 1, jnp.where(n < 7, 0, late_stop))
            group = jnp.where(i == 1, x, 1 - x)

            def step(at, carry):
                pool(at, group)
                return carry

            lax.fori_loop(start, stop, step, 0)

            @pl.when(jnp.logical_and(n == 11, i == 0))
            def _():
                sums_to.start()

    row_32 = lax.broadcasted_iota(jnp.int32, (32, 128), 0)
    length_of = jnp.ones((32, 128), jnp.float32)
    for b in range(8):
        for j in range(3):
            length_of = jnp.where(row_32 == b % 2 * 16 + b // 2 * 4 + j, meta_all[b, 4 + j:5 + j, :], length_of)
    length_wide = jnp.concatenate([length_of] * 4, axis=1)
    sums_to.wait_recv()
    doc_send[...] = ((pooled[x] + sums_in[...]) / length_wide).astype(jnp.bfloat16)

    def doc_to(i):
        return send(doc_send, doc_all.at[d], doc_s.at[i], doc_r.at[d], (v, (d + i) % 8))

    def doc_from(i):
        peer = (d + i) % 8
        return send(doc_send, doc_all.at[peer], doc_s.at[i], doc_r.at[peer], (v, peer))

    @pl.loop(1, 8)
    def _(i):
        doc_to(i).start()

    doc_all[d] = doc_send[...]

    length_sum = jnp.zeros((1, 128), jnp.float32)
    for b in range(8):
        for j in range(3):
            length_sum = length_sum + meta_all[b, 4 + j:5 + j, :]
    average = length_sum / 24.0
    den = saturate * (1.0 - length_slope + length_slope * length_of / average)
    den = jnp.concatenate([den] * 4, axis=1)
    own_queries.wait()

    @pl.loop(1, 8)
    def _(i):
        doc_from(i).wait_recv()

    pick_row = lax.broadcasted_iota(jnp.int32, (8, 32), 0)
    pick_col = lax.broadcasted_iota(jnp.int32, (8, 32), 1)
    pick = jnp.logical_and(pick_col == c * 16 + z * 4 + pick_row, pick_row < 3)
    pick = jnp.where(pick, 1.0, 0.0).astype(jnp.bfloat16)
    for b in range(8):
        cols = slice(b * 512, (b + 1) * 512)
        doc_out[:, cols] = jnp.dot(pick, doc_all[b], preferred_element_type=jnp.float32)
        weight = doc_all[b].astype(jnp.float32)
        scaled = weight * (saturate + 1.0) / (weight + den)
        masked[:, cols] = jnp.where(keep[:, cols] > 0.5, scaled, 0.0).astype(jnp.bfloat16)

    part[...] = lax.dot_general(
        masked[...], query_rows[...], (((1,), (1,)), ((), ())), preferred_element_type=jnp.float32
    )
    for zp in range(4):
        for side in range(2):
            part_send[zp, side * 4:side * 4 + 4, :] = part[side * 16 + zp * 4:side * 16 + zp * 4 + 4, :]

    def part_to(i):
        return send(part_send.at[(v + i) % 4], part_all.at[v], part_s.at[i], part_r.at[v], ((v + i) % 4, d))

    def part_from(i):
        peer = (v + i) % 4
        return send(part_send.at[peer], part_all.at[peer], part_s.at[i], part_r.at[peer], (peer, d))

    for i in range(1, 4):
        part_to(i).start()
    part_all[v] = part_send[v]

    side_terms.wait_send()
    sums_to.wait_send()

    @pl.loop(0, 12)
    def _(m):
        zp, j = m // 3, m % 3
        crossed = jnp.logical_and(y_first(j), zp != z)
        for side, there in ((y, True), (1 - y, y_first(j))):
            @pl.when(jnp.logical_and(there, jnp.logical_and(z < 3, zp <= z)))
            def _():
                go_up(m, side).wait_send()

            @pl.when(jnp.logical_and(there, jnp.logical_and(z > 0, zp >= z)))
            def _():
                go_down(m, side).wait_send()

        @pl.when(jnp.logical_not(crossed))
        def _():
            go_y(m).wait_send()

        go_sibling(m, 0).wait_send()
        go_sibling(m, 1).wait_send()

    @pl.loop(1, 8)
    def _(i):
        meta_to(i).wait_send()

    @pl.loop(1, 8)
    def _(i):
        doc_to(i).wait_send()

    for i in range(1, 4):
        part_from(i).wait_recv()
        part_to(i).wait_send()
    score_out[...] = (part_all[0] + part_all[1]) + (part_all[2] + part_all[3])


def local_kernel(hidden, w_vocab, lengths, query_terms, tile_routes):
    routes = jnp.pad(tile_routes[0].T.astype(jnp.float32), ((0, 0), (0, 96)))
    lens = jnp.broadcast_to(lengths.astype(jnp.float32)[:, None], (3, 128))
    meta = jnp.concatenate([routes, lens, jnp.zeros((1, 128), jnp.float32)], axis=0)
    width = hidden.shape[2]
    any_space, vmem = pl.BlockSpec(memory_space=pl.ANY), pl.BlockSpec(memory_space=pltpu.VMEM)
    dma = lambda count: pltpu.SemaphoreType.DMA((count,))
    docs, scores = pl.pallas_call(
        head_kernel,
        out_shape=(
            jax.ShapeDtypeStruct((8, 4096), jnp.float32),
            jax.ShapeDtypeStruct((8, 128), jnp.float32),
        ),
        in_specs=[any_space, any_space, any_space, vmem],
        out_specs=(vmem, vmem),
        scratch_shapes=[
            pltpu.VMEM((12, 256, width), jnp.bfloat16),
            pltpu.VMEM((2, 512, width), jnp.bfloat16),
            pltpu.VMEM((2, width, 512), jnp.bfloat16),
            pltpu.VMEM((128, 4096), jnp.bfloat16),
            pltpu.VMEM((8, 8, 128), jnp.float32),
            pltpu.VMEM((32, 4096), jnp.float32),
            pltpu.VMEM((2, 32, 512), jnp.float32),
            pltpu.VMEM((32, 512), jnp.bfloat16),
            pltpu.VMEM((8, 32, 512), jnp.bfloat16),
            pltpu.VMEM((32, 4096), jnp.bfloat16),
            pltpu.VMEM((32, 128), jnp.float32),
            pltpu.VMEM((4, 8, 128), jnp.float32),
            pltpu.VMEM((4, 8, 128), jnp.float32),
            pltpu.VMEM((32, 512), jnp.float32),
            dma(5), dma(1), dma(1), dma(24), dma(24), dma(24), dma(12), dma(12), dma(24), dma(24),
            dma(8), dma(8), dma(8), dma(8), dma(4), dma(4), dma(1), dma(1),
        ],
        compiler_params=pltpu.CompilerParams(
            collective_id=0, has_side_effects=True, vmem_limit_bytes=60 * 1024 * 1024
        ),
    )(hidden, w_vocab, query_terms, meta)
    doc_terms = docs[:3].astype(jnp.bfloat16)
    return doc_terms, scores.reshape(2, 4, 128)[:, :3].reshape(6, 128).T


def solution(mesh):
    shape = dict(mesh.shape)
    body = local_kernel if (shape["vocab"], shape["docs"]) == (4, 8) else local
    return jax.shard_map(
        body,
        mesh=mesh,
        in_specs=(
            P("docs", "vocab", None),
            P(("vocab", "docs"), None),
            P("docs"),
            P("docs", "vocab"),
            P("docs", "vocab", None),
        ),
        out_specs=(P("docs", "vocab"), P("docs", "vocab")),
        check_vma=False,
    )
```

```python
import jax
import jax.numpy as jnp
from jax import lax
from jax.experimental import pallas as pl
from jax.experimental.pallas import tpu as pltpu
from jax.sharding import PartitionSpec as P

saturate = 1.2
length_slope = 0.75


def pooled_rows(passage_rows, weights, lens_here):
    logits = lax.dot_general(
        passage_rows, weights, (((2,), (1,)), ((), ())), preferred_element_type=jnp.float32
    )
    places = lax.broadcasted_iota(jnp.int32, logits.shape, 1)
    activity = jnp.where(
        places < lens_here[:, None, None], jnp.log1p(jnp.maximum(logits, 0.0)), 0.0
    )
    return jnp.sum(activity, axis=1) / lens_here.astype(jnp.float32)[:, None]


def local(hidden, w_vocab, lengths, query_terms, tile_routes):
    members = lax.axis_size("docs")
    local_count = hidden.shape[0]
    lens_all = lax.all_gather(lengths, "docs", axis=0, tiled=True)
    passage_total = lens_all.shape[0]
    average = jnp.sum(lens_all.astype(jnp.float32)) / passage_total
    full_rows = lax.all_gather(hidden, "vocab", axis=1, tiled=True)
    doc_terms = pooled_rows(
        full_rows, lax.all_gather(w_vocab, "docs", axis=0, tiled=True), lengths
    ).astype(jnp.bfloat16)
    weight = doc_terms.astype(jnp.float32)
    denominator = saturate * (
        1.0 - length_slope + length_slope * lengths.astype(jnp.float32) / average
    )
    scaled = (weight * (saturate + 1.0) / (weight + denominator[:, None])).astype(jnp.bfloat16)
    term_count = scaled.shape[1]
    tile_count = term_count // 128
    my_routes = tile_routes[0]
    fanout = my_routes.shape[1]
    capacity = min(tile_count, max(4, 2 * tile_count * fanout // members))
    owners = lax.broadcasted_iota(jnp.int32, (1, 1, members), 2)
    is_listed = jnp.any(my_routes[:, :, None] == owners, axis=1)
    slot_index = jnp.cumsum(is_listed.astype(jnp.int32), axis=0) - 1
    slot_ids = lax.broadcasted_iota(jnp.int32, (1, capacity, 1), 1)
    selector = (is_listed.T[:, None, :] & (slot_index.T[:, None, :] == slot_ids)).astype(
        jnp.bfloat16
    )
    blocks = scaled.reshape(local_count, tile_count, 128)
    outgoing = jnp.einsum(
        "oct,ptk->ocpk", selector, blocks, preferred_element_type=jnp.float32
    ).astype(jnp.bfloat16)
    tile_ids = lax.broadcasted_iota(jnp.float32, (1, 1, tile_count), 2)
    labels = jnp.sum(selector.astype(jnp.float32) * tile_ids, axis=2).astype(jnp.bfloat16)
    arrived, labels_in = (
        lax.all_to_all(outgoing, "docs", split_axis=0, concat_axis=0, tiled=True),
        lax.all_to_all(labels, "docs", split_axis=0, concat_axis=0, tiled=True),
    )
    placing = (labels_in.astype(jnp.float32)[:, :, None] == tile_ids).astype(jnp.bfloat16)
    masked = jnp.einsum(
        "bct,bcpk->bptk", placing, arrived, preferred_element_type=jnp.float32
    ).astype(jnp.bfloat16)
    masked = masked.reshape(passage_total, term_count)
    partial_value = lax.dot_general(
        query_terms, masked, (((1,), (1,)), ((), ())), preferred_element_type=jnp.float32
    )
    scores = lax.psum_scatter(partial_value, "vocab", scatter_dimension=1, tiled=True)
    return (doc_terms, scores)


CHUNK = 256
MESH = pl.DeviceIdType.MESH


def head_kernel(
    hidden, weights, queries, meta, doc_out, score_out,
    rows, terms, turned, query_rows, meta_all, keep, pooled, doc_send, doc_all, masked, part, part_send, part_all, sums_in,
    local_sem, w_s, w_r, up_s, down_s, z_r, y_s, y_r, sib_s, sib_r,
    meta_s, meta_r, doc_s, doc_r, part_s, part_r, sum_s, sum_r,
):
    v, d = lax.axis_index("vocab"), lax.axis_index("docs")
    x, y, z, c = v % 2, v // 2, d // 2, d % 2
    x_side, y_side = (2 * y + 1 - x, d), (2 * (1 - y) + x, d)
    sibling = (v, 2 * z + 1 - c)
    above, below = (v, d + 2), (v, d - 2)

    def send(src, dst, s_sem, r_sem, to):
        return pltpu.make_async_remote_copy(
            src_ref=src, dst_ref=dst, send_sem=s_sem, recv_sem=r_sem, device_id=to, device_id_type=MESH
        )

    barrier = pltpu.get_barrier_semaphore()

    @pl.loop(1, 8)
    def _(i):
        pl.semaphore_signal(barrier, inc=1, device_id=(v, (d + i) % 8), device_id_type=MESH)

    for i in range(1, 4):
        pl.semaphore_signal(barrier, inc=1, device_id=((v + i) % 4, d), device_id_type=MESH)
    pl.semaphore_wait(barrier, 10)

    def slot(m, vp):
        return rows.at[m, pl.ds(pl.multiple_of(vp * 64, 64), 64), :]

    def own_rows(j):
        return pltpu.make_async_copy(hidden.at[j], slot(z * 3 + j, 2 * c + y), local_sem.at[j])

    own_terms = pltpu.make_async_copy(weights, terms.at[x], local_sem.at[3])
    own_queries = pltpu.make_async_copy(queries, query_rows, local_sem.at[4])

    side_terms = send(weights, terms.at[x], w_s.at[0], w_r.at[0], x_side)
    side_terms_in = send(weights, terms.at[1 - x], w_s.at[0], w_r.at[0], x_side)

    def go_up(m, side):
        block, at = slot(m, 2 * c + side), m * 2 + side
        return send(block, block, up_s.at[at], z_r.at[at], above)

    def go_down(m, side):
        block, at = slot(m, 2 * c + side), m * 2 + side
        return send(block, block, down_s.at[at], z_r.at[at], below)

    items = 4 - c

    def item(at):
        extra = at % items == 3
        return jnp.where(extra, 0, (at % items + 1) % 3), jnp.where(extra, 1 - y, y)

    def send_z(at):
        far = at // items
        j, side = item(at)

        @pl.when(jnp.logical_and(z < 3, z - far >= 0))
        def _():
            go_up((z - far) * 3 + j, side).start()

        @pl.when(jnp.logical_and(z > 0, z + far <= 3))
        def _():
            go_down((z + far) * 3 + j, side).start()

    def y_first(j):
        return jnp.logical_and(c == 0, j == 0)

    def go_y(m):
        return send(slot(m, 2 * c + y), slot(m, 2 * c + y), y_s.at[m], y_r.at[m], y_side)

    def come_y(m):
        block = slot(m, 2 * c + 1 - y)
        return send(block, block, y_s.at[m], y_r.at[m], y_side)

    def go_sibling(m, side):
        block = slot(m, 2 * c + side)
        return send(block, block, sib_s.at[m * 2 + side], sib_r.at[m * 2 + side], sibling)

    def come_sibling(m, side):
        block = slot(m, 2 * (1 - c) + side)
        return send(block, block, sib_s.at[m * 2 + side], sib_r.at[m * 2 + side], sibling)

    for j in range(3):
        own_rows(j).start()
    side_terms.start()

    def meta_to(i):
        peer = (d + i) % 8
        return send(meta, meta_all.at[d], meta_s.at[i], meta_r.at[d], (v, peer))

    def meta_from(i):
        peer = (d + i) % 8
        return send(meta, meta_all.at[peer], meta_s.at[i], meta_r.at[peer], (v, peer))

    @pl.loop(1, 8)
    def _(i):
        meta_to(i).start()

    meta_all[d] = meta[...]
    own_terms.start()
    own_queries.start()
    pooled[...] = jnp.zeros_like(pooled)

    for j in range(3):
        own_rows(j).wait()
    for j in range(2):
        send_z(j)
        go_y(z * 3 + j).start()
    for j in range(3):
        go_sibling(z * 3 + j, y).start()

    own_terms.wait()
    turned[x] = terms[x].T

    @pl.loop(1, 8)
    def _(i):
        meta_from(i).wait_recv()

    row_id = lax.broadcasted_iota(jnp.int32, (16, 128), 0)
    mine = d.astype(jnp.float32)
    for side in range(2):
        listed = jnp.zeros((16, 128), jnp.float32)
        for zp in range(4):
            routes = meta_all[2 * zp + side][0:4, :]
            hit = jnp.max(jnp.where(routes == mine, 1.0, 0.0), axis=0, keepdims=True)
            listed = jnp.where(row_id // 4 == zp, hit, listed)
        for t in range(32):
            keep[side * 16:side * 16 + 16, t * 128:(t + 1) * 128] = jnp.broadcast_to(listed[:, t:t + 1], (16, 128))

    def order(n):
        end = jnp.logical_or(z == 0, z == 3)
        step = n - 3
        end_z = jnp.where(z == 0, z + step // 3 + 1, z - step // 3 - 1)
        near = jnp.where(step % 2 == 0, z - 1, z + 1)
        mid_z = jnp.where(n < 9, near, jnp.where(z == 1, 3, 0))
        mid_j = jnp.where(n < 9, step // 2, n - 9)
        zp = jnp.where(n < 3, z, jnp.where(end, end_z, mid_z))
        j = jnp.where(n < 3, n, (jnp.where(end, step % 3, mid_j) + 1) % 3)
        return zp, j

    place = lax.broadcasted_iota(jnp.int32, (8, CHUNK), 0).astype(jnp.float32)

    def pool(zp, group):
        for half in range(0, 512, CHUNK):
            block = rows[pl.ds(zp * 3, 3)].reshape(768, rows.shape[2])
            logits = jnp.dot(block, turned[group, :, half:half + CHUNK], preferred_element_type=jnp.float32)
            for core in range(2):
                for j in range(3):
                    length = meta_all[2 * zp + core, 4 + j:5 + j, :]
                    length = jnp.concatenate([length] * (CHUNK // 128), axis=1)
                    total = jnp.zeros((8, CHUNK), jnp.float32)
                    for side in range(2):
                        room = length - place - (64 * x + 128 * side).astype(jnp.float32)
                        at = 256 * j + 128 * core + 64 * side
                        parts = [
                            jnp.where(room > float(8 * i), jnp.maximum(logits[at + 8 * i:at + 8 * i + 8, :], 0.0), 0.0)
                            for i in range(8)
                        ]
                        while len(parts) > 1:
                            parts = [a + b + a * b for a, b in zip(parts[0::2], parts[1::2])]
                        total = total + jnp.log1p(parts[0])
                    row = pl.ds(core * 16 + zp * 4 + j, 1)
                    pooled[group, row, half:half + CHUNK] = jnp.sum(total, axis=0, keepdims=True)

    sums_to = send(pooled.at[1 - x], sums_in, sum_s.at[0], sum_r.at[0], x_side)

    def crosses(zp, j):
        return jnp.logical_or(jnp.logical_not(y_first(j)), zp == z)

    @pl.loop(0, 12)
    def _(n):
        zp, jj = order(n)
        m = zp * 3 + jj

        @pl.when(crosses(zp, jj))
        def _():
            come_y(m).wait_recv()
            go_sibling(m, 1 - y).start()

        far = n // items + 1
        j, side = item(n)

        @pl.when(z - far >= 0)
        def _():
            at = (z - far) * 3 + j
            go_up(at, side).wait_recv()
            go_sibling(at, side).start()

        @pl.when(z + far <= 3)
        def _():
            at = (z + far) * 3 + j
            go_down(at, side).wait_recv()
            go_sibling(at, side).start()

        send_z(n + 2)
        ahead = jnp.where(jnp.logical_and(c == 0, n > 7), n + 1, n + 2)
        skip = jnp.logical_and(c == 0, n == 7)
        next_z, next_j = order(ahead)
        crossing = jnp.logical_and(ahead < 12, crosses(next_z, next_j))

        @pl.when(jnp.logical_and(crossing, jnp.logical_not(skip)))
        def _():
            go_y(next_z * 3 + next_j).start()

        come_sibling(m, 0).wait_recv()
        come_sibling(m, 1).wait_recv()

        @pl.when(n == 7)
        def _():
            side_terms_in.wait_recv()
            turned[1 - x] = terms[1 - x].T

        @pl.loop(0, 2)
        def _(i):
            turn = jnp.where(i == 1, n, jnp.where(n < 7, 0, jnp.where(n == 7, 2, jnp.where(n == 8, 5, jnp.where(n == 11, 11, n - 1)))))
            at_end = jnp.where(z == 0, turn // 3, 3 - turn // 3)
            at_mid = jnp.where(turn == 2, z, jnp.where(turn == 8, z - 1, jnp.where(turn == 9, z + 1, jnp.where(z == 1, 3, 0))))
            end = jnp.logical_or(z == 0, z == 3)
            due_end = turn % 3 == 2
            due_mid = jnp.logical_or(jnp.logical_or(turn == 2, turn == 8), jnp.logical_or(turn == 9, turn == 11))
            due = jnp.where(end, due_end, due_mid)
            group = jnp.where(i == 1, x, 1 - x)

            @pl.when(due)
            def _():
                pool(jnp.where(end, at_end, at_mid), group)

            @pl.when(jnp.logical_and(n == 11, i == 0))
            def _():
                sums_to.start()

    row_32 = lax.broadcasted_iota(jnp.int32, (32, 128), 0)
    length_of = jnp.ones((32, 128), jnp.float32)
    for b in range(8):
        for j in range(3):
            length_of = jnp.where(row_32 == b % 2 * 16 + b // 2 * 4 + j, meta_all[b, 4 + j:5 + j, :], length_of)
    length_wide = jnp.concatenate([length_of] * 4, axis=1)
    sums_to.wait_recv()
    doc_send[...] = ((pooled[x] + sums_in[...]) / length_wide).astype(jnp.bfloat16)

    def doc_to(i):
        return send(doc_send, doc_all.at[d], doc_s.at[i], doc_r.at[d], (v, (d + i) % 8))

    def doc_from(i):
        peer = (d + i) % 8
        return send(doc_send, doc_all.at[peer], doc_s.at[i], doc_r.at[peer], (v, peer))

    @pl.loop(1, 8)
    def _(i):
        doc_to(i).start()

    doc_all[d] = doc_send[...]

    length_sum = jnp.zeros((1, 128), jnp.float32)
    for b in range(8):
        for j in range(3):
            length_sum = length_sum + meta_all[b, 4 + j:5 + j, :]
    average = length_sum / 24.0
    den = saturate * (1.0 - length_slope + length_slope * length_of / average)
    den = jnp.concatenate([den] * 4, axis=1)
    own_queries.wait()

    @pl.loop(1, 8)
    def _(i):
        doc_from(i).wait_recv()

    pick_row = lax.broadcasted_iota(jnp.int32, (8, 32), 0)
    pick_col = lax.broadcasted_iota(jnp.int32, (8, 32), 1)
    pick = jnp.logical_and(pick_col == c * 16 + z * 4 + pick_row, pick_row < 3)
    pick = jnp.where(pick, 1.0, 0.0).astype(jnp.bfloat16)
    for b in range(8):
        cols = slice(b * 512, (b + 1) * 512)
        doc_out[:, cols] = jnp.dot(pick, doc_all[b], preferred_element_type=jnp.float32)
        weight = doc_all[b].astype(jnp.float32)
        scaled = weight * (saturate + 1.0) / (weight + den)
        masked[:, cols] = jnp.where(keep[:, cols] > 0.5, scaled, 0.0).astype(jnp.bfloat16)

    part[...] = lax.dot_general(
        masked[...], query_rows[...], (((1,), (1,)), ((), ())), preferred_element_type=jnp.float32
    )
    for zp in range(4):
        for side in range(2):
            part_send[zp, side * 4:side * 4 + 4, :] = part[side * 16 + zp * 4:side * 16 + zp * 4 + 4, :]

    def part_to(i):
        return send(part_send.at[(v + i) % 4], part_all.at[v], part_s.at[i], part_r.at[v], ((v + i) % 4, d))

    def part_from(i):
        peer = (v + i) % 4
        return send(part_send.at[peer], part_all.at[peer], part_s.at[i], part_r.at[peer], (peer, d))

    for i in range(1, 4):
        part_to(i).start()
    part_all[v] = part_send[v]

    side_terms.wait_send()
    sums_to.wait_send()

    @pl.loop(0, 12)
    def _(m):
        zp, j = m // 3, m % 3
        crossed = jnp.logical_and(y_first(j), zp != z)
        for side, there in ((y, True), (1 - y, y_first(j))):
            @pl.when(jnp.logical_and(there, jnp.logical_and(z < 3, zp <= z)))
            def _():
                go_up(m, side).wait_send()

            @pl.when(jnp.logical_and(there, jnp.logical_and(z > 0, zp >= z)))
            def _():
                go_down(m, side).wait_send()

        @pl.when(jnp.logical_not(crossed))
        def _():
            go_y(m).wait_send()

        go_sibling(m, 0).wait_send()
        go_sibling(m, 1).wait_send()

    @pl.loop(1, 8)
    def _(i):
        meta_to(i).wait_send()

    @pl.loop(1, 8)
    def _(i):
        doc_to(i).wait_send()

    for i in range(1, 4):
        part_from(i).wait_recv()
        part_to(i).wait_send()
    score_out[...] = (part_all[0] + part_all[1]) + (part_all[2] + part_all[3])


def local_kernel(hidden, w_vocab, lengths, query_terms, tile_routes):
    routes = jnp.pad(tile_routes[0].T.astype(jnp.float32), ((0, 0), (0, 96)))
    lens = jnp.broadcast_to(lengths.astype(jnp.float32)[:, None], (3, 128))
    meta = jnp.concatenate([routes, lens, jnp.zeros((1, 128), jnp.float32)], axis=0)
    width = hidden.shape[2]
    any_space, vmem = pl.BlockSpec(memory_space=pl.ANY), pl.BlockSpec(memory_space=pltpu.VMEM)
    dma = lambda count: pltpu.SemaphoreType.DMA((count,))
    docs, scores = pl.pallas_call(
        head_kernel,
        out_shape=(
            jax.ShapeDtypeStruct((8, 4096), jnp.float32),
            jax.ShapeDtypeStruct((8, 128), jnp.float32),
        ),
        in_specs=[any_space, any_space, any_space, vmem],
        out_specs=(vmem, vmem),
        scratch_shapes=[
            pltpu.VMEM((12, 256, width), jnp.bfloat16),
            pltpu.VMEM((2, 512, width), jnp.bfloat16),
            pltpu.VMEM((2, width, 512), jnp.bfloat16),
            pltpu.VMEM((128, 4096), jnp.bfloat16),
            pltpu.VMEM((8, 8, 128), jnp.float32),
            pltpu.VMEM((32, 4096), jnp.float32),
            pltpu.VMEM((2, 32, 512), jnp.float32),
            pltpu.VMEM((32, 512), jnp.bfloat16),
            pltpu.VMEM((8, 32, 512), jnp.bfloat16),
            pltpu.VMEM((32, 4096), jnp.bfloat16),
            pltpu.VMEM((32, 128), jnp.float32),
            pltpu.VMEM((4, 8, 128), jnp.float32),
            pltpu.VMEM((4, 8, 128), jnp.float32),
            pltpu.VMEM((32, 512), jnp.float32),
            dma(5), dma(1), dma(1), dma(24), dma(24), dma(24), dma(12), dma(12), dma(24), dma(24),
            dma(8), dma(8), dma(8), dma(8), dma(4), dma(4), dma(1), dma(1),
        ],
        compiler_params=pltpu.CompilerParams(
            collective_id=0, has_side_effects=True, vmem_limit_bytes=60 * 1024 * 1024
        ),
    )(hidden, w_vocab, query_terms, meta)
    doc_terms = docs[:3].astype(jnp.bfloat16)
    return doc_terms, scores.reshape(2, 4, 128)[:, :3].reshape(6, 128).T


def solution(mesh):
    shape = dict(mesh.shape)
    body = local_kernel if (shape["vocab"], shape["docs"]) == (4, 8) else local
    return jax.shard_map(
        body,
        mesh=mesh,
        in_specs=(
            P("docs", "vocab", None),
            P(("vocab", "docs"), None),
            P("docs"),
            P("docs", "vocab"),
            P("docs", "vocab", None),
        ),
        out_specs=(P("docs", "vocab"), P("docs", "vocab")),
        check_vma=False,
    )
```
